256 devices in a mesh: row: 16 (over z, core), col: 16 (over y, x).
Axes of the slice: x: 4, y: 4, z: 8, core: 2. Of those that a mesh axis runs over, the one named last changes fastest.
Arguments:
- patches: bfloat16 [16, 16, 2, 16, 128, 128], P('row', 'col'), as said below
- windows: bfloat16 [16, 16, 2, 16, 36864], P('row', 'col'), as said below
- candidates: int32 [16, 16, 2, 2, 128], P('row', 'col'), may hold values from -32 to 32, as said below
- live: int32 [16, 16, 2], replicated, may hold values from 1 to 16, as said below
- edges: int32 [16, 2, 11280], P('row', None, 'col'), may hold values from 0 to 255, as said below
- stiffness: float32 [16, 11280], P('row', 'col'), may hold values from 0.3 to 3
Outputs:
- matches: float32 [16, 16, 2, 3, 16], P('row', 'col')
- mesh_shift: float32 [16, 16, 2, 256], P('row', 'col')
The draws below stay inside these ranges and needn't reach their ends.
Inputs may be any that keep to these rules, and one draw needn't show every extreme that they name: `candidates`: the candidate shifts of a patch need not be distinct. live[r, c, k] counts the live slots of seam k of tile (r, c): slots 0 to live - 1; the same for all devices. Each tile's springs are the edges of its 16 x 16 vertex grid, horizontal and vertical, and one diagonal of every cell, in any order. `windows`: window k of tile (r, c) serves the seam that tile (r, c-1) (k = 0) or tile (r-1, c) (k = 1) holds as its seam k. `patches`: patch p of seam k is scored against window p of the neighbour.
All inputs are finite; a program needn't handle non-finite values.
Results may differ from the reference program's by a relative error of at most 0.0003.
Values may be sent and summed in bfloat16 or wider, within the bound.
No kernel may reach another device: no remote copies, remote signals or barrier semaphores. Data moves between devices by JAX's collectives and lax.ppermute only.
A program may use at most 64 MiB of HBM per device.

```python
import math
import jax
import jax.numpy as jnp
from jax import lax

PATCH = 128
REACH = 32
WIN = 192
NS = 8
P_SIZE = 16
GV = 16
E = 705
ITERS = 3
TILE_ROWS = 16
TILE_COLS = 16


def window_frame(key, flat_index):
    frame_key = jax.random.fold_in(jax.random.fold_in(key, 101), flat_index)
    return jax.random.normal(frame_key, (WIN, WIN), jnp.float32)


def shift_table(key):
    table_total = TILE_ROWS * TILE_COLS * 2 * 2 * P_SIZE * NS
    values = jax.random.randint(jax.random.fold_in(key, 202), (table_total,), -REACH, REACH + 1)
    half_way = table_total // 2
    high_spot = jax.random.randint(jax.random.fold_in(key, 203), (), 0, half_way)
    low_spot = jax.random.randint(jax.random.fold_in(key, 204), (), half_way, table_total)
    values = values.at[high_spot].set(REACH).at[low_spot].set(-REACH)
    return values.reshape(TILE_ROWS, TILE_COLS, 2, 2, P_SIZE * NS).astype(jnp.int32)


def draw_windows(key, part):

    def one_frame(flat_index):
        return window_frame(key, flat_index).astype(jnp.bfloat16).reshape(WIN * WIN)
    frames = lax.map(one_frame, jnp.arange(TILE_ROWS * TILE_COLS * 2 * P_SIZE, dtype=jnp.int32))
    return frames.reshape(TILE_ROWS, TILE_COLS, 2, P_SIZE, WIN * WIN)


def draw_candidates(key, part):
    return shift_table(key)


def draw_patches(key, part):
    shifts = shift_table(key)
    truth = jax.random.randint(jax.random.fold_in(key, 303), (TILE_ROWS, TILE_COLS, 2, P_SIZE), 0, NS)

    def one_patch(flat_index):
        slot_index = flat_index % P_SIZE
        rest_index = flat_index // P_SIZE
        seam = rest_index % 2
        tile_index = rest_index // 2
        tile_row = tile_index // TILE_COLS
        tile_col = tile_index % TILE_COLS
        near_row = (tile_row + seam) % TILE_ROWS
        near_col = (tile_col + 1 - seam) % TILE_COLS
        near_index = ((near_row * TILE_COLS + near_col) * 2 + seam) * P_SIZE + slot_index
        frame_values = window_frame(key, near_index)
        chosen = truth[tile_row, tile_col, seam, slot_index]
        move_y = shifts[tile_row, tile_col, seam, 0, slot_index * NS + chosen]
        move_x = shifts[tile_row, tile_col, seam, 1, slot_index * NS + chosen]
        cropped = lax.dynamic_slice(frame_values, (REACH + move_y, REACH + move_x), (PATCH, PATCH))
        noise = jax.random.normal(jax.random.fold_in(jax.random.fold_in(key, 404), flat_index), (PATCH, PATCH), jnp.float32)
        return (0.8 * cropped + 0.6 * noise).astype(jnp.bfloat16)
    made = lax.map(one_patch, jnp.arange(TILE_ROWS * TILE_COLS * 2 * P_SIZE, dtype=jnp.int32))
    return made.reshape(TILE_ROWS, TILE_COLS, 2, P_SIZE, PATCH, PATCH)


def draw_live(key, part):
    columns = jnp.arange(TILE_COLS, dtype=jnp.int32)
    low_end = max(P_SIZE // 4, 1)
    ramp = low_end + (P_SIZE - low_end) * columns // max(TILE_COLS - 1, 1)
    lowered = jax.random.randint(jax.random.fold_in(key, 505), (TILE_ROWS, TILE_COLS, 2), 0, low_end + 1)
    counts = jnp.clip(ramp[None, :, None] - lowered, 1, P_SIZE)
    top_row = jax.random.randint(jax.random.fold_in(key, 506), (), 0, TILE_ROWS)
    top_col = jax.random.randint(jax.random.fold_in(key, 507), (), 1, TILE_COLS)
    low_row = jax.random.randint(jax.random.fold_in(key, 508), (), 0, TILE_ROWS)
    counts = counts.at[low_row, 0, :].set(1).at[top_row, top_col, :].set(P_SIZE)
    return counts.astype(jnp.int32)


def draw_edges(key, part):
    grid = jnp.arange(GV * GV, dtype=jnp.int32).reshape(GV, GV)
    cells = TILE_ROWS * TILE_COLS
    flip = jax.random.randint(jax.random.fold_in(key, 601), (cells, (GV - 1) * (GV - 1)), 0, 2)
    diag_first = jnp.where(flip == 1, grid[:-1, 1:].reshape(-1)[None, :], grid[:-1, :-1].reshape(-1)[None, :])
    diag_second = jnp.where(flip == 1, grid[1:, :-1].reshape(-1)[None, :], grid[1:, 1:].reshape(-1)[None, :])
    fixed_first = jnp.concatenate([grid[:, :-1].reshape(-1), grid[:-1, :].reshape(-1)])
    fixed_second = jnp.concatenate([grid[:, 1:].reshape(-1), grid[1:, :].reshape(-1)])
    first_ends = jnp.concatenate([jnp.broadcast_to(fixed_first[None, :], (cells, fixed_first.shape[0])), diag_first], axis=1)
    second_ends = jnp.concatenate([jnp.broadcast_to(fixed_second[None, :], (cells, fixed_second.shape[0])), diag_second], axis=1)

    def one_order(order_key):
        return jax.random.permutation(order_key, E)
    orders = jax.vmap(one_order)(jax.random.split(jax.random.fold_in(key, 602), cells))
    first_ends = jnp.take_along_axis(first_ends, orders, axis=1)
    second_ends = jnp.take_along_axis(second_ends, orders, axis=1)
    paired = jnp.stack([first_ends, second_ends], axis=1)
    paired = paired.reshape(TILE_ROWS, TILE_COLS, 2, E).transpose(0, 2, 1, 3)
    return paired.reshape(TILE_ROWS, 2, TILE_COLS * E).astype(jnp.int32)


def block_scale(rng, shape, cuts, low, high):
    gain = 1.0
    for position, blocks in cuts:
        draws = jax.random.uniform(jax.random.fold_in(jax.random.fold_in(rng, 6), position), (blocks,), jnp.float32, low / len(cuts), high / len(cuts))
        gain = gain * jnp.repeat(jnp.exp(draws), shape[position] // blocks).reshape((-1,) + (1,) * (len(shape) - 1 - position))
    return gain


def setup_inputs(seed: int = 0) -> dict:
    splits = jax.random.split(jax.random.key(seed), 7)
    return {
        "patches": draw_patches(jax.random.fold_in(splits[6], 71), 0),
        "windows": draw_windows(jax.random.fold_in(splits[6], 71), 0),
        "candidates": draw_candidates(jax.random.fold_in(splits[6], 71), 0),
        "live": draw_live(jax.random.fold_in(splits[6], 71), 0),
        "edges": draw_edges(jax.random.fold_in(splits[6], 71), 0),
        "stiffness": jnp.clip(jnp.exp(math.log(3.0) - 2.3025851 * jax.random.uniform(splits[5], (TILE_ROWS, TILE_COLS * E), jnp.float32) ** block_scale(splits[5], (TILE_ROWS, TILE_COLS * E), ((0, 16), (1, 16)), -0.2, 0.2)), 0.3, 3.0),
    }


LAMBDA_REG = 0.05
EPSILON = 1e-05
PRECISE = lax.Precision.HIGHEST

def match_block(patch_raw, frames, list_y, list_x):
    patch_size = patch_raw.shape[-1]
    cand_count = list_y.shape[-1]
    pixel_count = float(patch_size * patch_size)
    frame_pixels_all = frames.reshape(frames.shape[0], WIN, WIN)

    def crop_all(frame_pixels, shifts_y, shifts_x):

        def crop_one(move_y, move_x):
            return lax.dynamic_slice(frame_pixels, (REACH + move_y, REACH + move_x), (patch_size, patch_size))
        return jax.vmap(crop_one)(shifts_y, shifts_x)
    cropped = jax.vmap(crop_all)(frame_pixels_all, list_y, list_x)
    unit_plane = jnp.ones((patch_size, patch_size), patch_raw.dtype)
    patch_sum = jnp.einsum('byx,yx->b', patch_raw, unit_plane, preferred_element_type=jnp.float32)
    patch_square = jnp.einsum('byx,byx->b', patch_raw, patch_raw, preferred_element_type=jnp.float32)
    crop_sum = jnp.einsum('bsyx,yx->bs', cropped, unit_plane, preferred_element_type=jnp.float32)
    crop_square = jnp.einsum('bsyx,bsyx->bs', cropped, cropped, preferred_element_type=jnp.float32)
    cross_sum = jnp.einsum('byx,bsyx->bs', patch_raw, cropped, preferred_element_type=jnp.float32)
    patch_mean = patch_sum / pixel_count
    crop_mean = crop_sum / pixel_count
    patch_var = patch_square / pixel_count - patch_mean * patch_mean
    crop_var = crop_square / pixel_count - crop_mean * crop_mean
    cross_mean = cross_sum / pixel_count - patch_mean[:, None] * crop_mean
    correl = cross_mean / jnp.sqrt((patch_var[:, None] + EPSILON) * (crop_var + EPSILON))
    weight = (1.5 + correl) * (1.5 + correl)
    weight_sum = lax.optimization_barrier(jnp.sum(weight, axis=1))
    along_y = lax.optimization_barrier(jnp.sum(weight * list_y.astype(jnp.float32), axis=1)) / (REACH * weight_sum)
    along_x = lax.optimization_barrier(jnp.sum(weight * list_x.astype(jnp.float32), axis=1)) / (REACH * weight_sum)
    return jnp.stack([along_y, along_x, weight_sum / cand_count])

def reference(patches, windows, candidates, live, edges, stiffness):
    rows_all = TILE_ROWS
    cols_all = TILE_COLS
    slots = jnp.arange(P_SIZE)

    def tile_matches(flat_index):
        tile_row = flat_index // cols_all
        tile_col = flat_index % cols_all
        results = []
        for seam in range(2):
            near_row = jnp.minimum(tile_row + seam, rows_all - 1)
            near_col = jnp.minimum(tile_col + 1 - seam, cols_all - 1)
            exists = (tile_row + seam < rows_all) & (tile_col + 1 - seam < cols_all)
            live_count = jnp.where(exists, live[tile_row, tile_col, seam], 0)
            shift_grid = candidates[tile_row, tile_col, seam].reshape(2, P_SIZE, NS)
            scored = match_block(patches[tile_row, tile_col, seam], windows[near_row, near_col, seam], shift_grid[0], shift_grid[1])
            results.append(scored * (slots < live_count).astype(jnp.float32))
        return jnp.stack(results)
    matches = lax.map(tile_matches, jnp.arange(rows_all * cols_all, dtype=jnp.int32))
    matches = matches.reshape(rows_all, cols_all, 2, 3, P_SIZE)
    picker = (jnp.arange(GV)[None, :] == (slots * GV // P_SIZE)[:, None]).astype(jnp.float32)

    def spread(values):
        return jnp.einsum('rcap,pg->rcag', values, picker, precision=PRECISE)

    def sample(values):
        return jnp.einsum('rcag,pg->rcap', values, picker, precision=PRECISE)

    def from_left(values):
        return jnp.concatenate([jnp.zeros_like(values[:, :1]), values[:, :-1]], axis=1)

    def from_right(values):
        return jnp.concatenate([values[:, 1:], jnp.zeros_like(values[:, :1])], axis=1)

    def from_above(values):
        return jnp.concatenate([jnp.zeros_like(values[:1]), values[:-1]], axis=0)

    def from_below(values):
        return jnp.concatenate([values[1:], jnp.zeros_like(values[:1])], axis=0)
    conf_east = matches[:, :, 0, 2][:, :, None]
    conf_south = matches[:, :, 1, 2][:, :, None]
    shift_east = matches[:, :, 0, :2]
    shift_south = matches[:, :, 1, :2]
    conf_west = from_left(conf_east)
    shift_west = from_left(shift_east)
    conf_north = from_above(conf_south)
    shift_north = from_above(shift_south)
    endpoints = edges.reshape(rows_all, 2, cols_all, E).transpose(0, 2, 1, 3)
    spring = stiffness.reshape(rows_all, cols_all, E)

    def intra_tile(flat_field, ends, strength):
        stretch = (flat_field[:, ends[0]] - flat_field[:, ends[1]]) * strength
        return jnp.zeros_like(flat_field).at[:, ends[0]].add(stretch).at[:, ends[1]].add(-stretch)
    intra = jax.vmap(jax.vmap(intra_tile))

    def operate(vector):
        flat_field = vector.reshape(rows_all, cols_all, 2, GV * GV)
        output = (LAMBDA_REG * flat_field + intra(flat_field, endpoints, spring)).reshape(vector.shape)
        output = output.at[..., :, GV - 1].add(spread(conf_east * sample(vector[..., :, GV - 1] - from_right(vector[..., :, 0]))))
        output = output.at[..., :, 0].add(spread(conf_west * sample(vector[..., :, 0] - from_left(vector[..., :, GV - 1]))))
        output = output.at[..., GV - 1, :].add(spread(conf_south * sample(vector[..., GV - 1, :] - from_below(vector[..., 0, :]))))
        output = output.at[..., 0, :].add(spread(conf_north * sample(vector[..., 0, :] - from_above(vector[..., GV - 1, :]))))
        return output
    forcing = jnp.zeros((rows_all, cols_all, 2, GV, GV), jnp.float32)
    forcing = forcing.at[..., :, GV - 1].add(spread(conf_east * shift_east))
    forcing = forcing.at[..., :, 0].add(-spread(conf_west * shift_west))
    forcing = forcing.at[..., GV - 1, :].add(spread(conf_south * shift_south))
    forcing = forcing.at[..., 0, :].add(-spread(conf_north * shift_north))
    solution = jnp.zeros_like(forcing)
    residual = forcing
    direction = forcing
    norm_now = jnp.sum(residual * residual)
    for iteration in range(ITERS):
        applied = operate(direction)
        step_length = norm_now / jnp.sum(direction * applied)
        solution = solution + step_length * direction
        residual = residual - step_length * applied
        norm_next = jnp.sum(residual * residual)
        direction = residual + norm_next / norm_now * direction
        norm_now = norm_next
    return (matches, solution.reshape(rows_all, cols_all, 2, GV * GV))
```

```python
import functools

import jax
import jax.numpy as jnp
from jax import lax
from jax.experimental import pallas as pl
from jax.experimental.pallas import tpu as pltpu
from jax.sharding import PartitionSpec as P

PATCH = 128
REACH = 32
WIN = 192
NS = 8
P_SIZE = 16
GV = 16
E = 705
E_PAD = 768
LINES = WIN * WIN // 128
PIXELS = float(PATCH * PATCH)
LAMBDA_REG = 0.05
EPSILON = 1e-05
THETA = 8.0
PRECISE = lax.Precision.HIGHEST
F32 = jnp.float32
VMEM = pl.BlockSpec(memory_space=pltpu.VMEM)
SMEM = pl.BlockSpec(memory_space=pltpu.SMEM)


def shifted(x, axis, by):
    length = lax.axis_size(axis)
    pairs = [(i, i + by) for i in range(length) if 0 <= i + by < length]
    return lax.ppermute(x, axis, pairs)


def iota(shape, dim):
    return lax.broadcasted_iota(jnp.int32, shape, dim)


def nt_dot(a, b):
    return lax.dot_general(
        a, b, (((1,), (1,)), ((), ())), precision=PRECISE, preferred_element_type=F32
    )


def frames_kernel(win_ref, out_ref):
    for seam in range(2):

        def one_line(j, carry, seam=seam):
            at = pl.multiple_of(j * 128, 128)
            pixels = win_ref[seam, :, pl.ds(at, 128)].astype(F32)
            base = seam * P_SIZE * LINES + j
            out_ref[pl.ds(base, 8, stride=LINES), :] = pixels[:8]
            out_ref[pl.ds(base + 8 * LINES, 8, stride=LINES), :] = pixels[8:]
            return carry

        lax.fori_loop(0, LINES, one_line, 0, unroll=8)


def springs_kernel(edges_ref, stiff_ref, out_ref, ends_scr, stiff_scr):
    ends_scr[...] = jnp.zeros_like(ends_scr)
    stiff_scr[...] = jnp.zeros_like(stiff_scr)
    ends_scr[0:2, 0:E] = edges_ref[...]
    stiff_scr[0:1, 0:E] = stiff_ref[...]
    first, second = ends_scr[0:1], ends_scr[1:2]
    strength = stiff_scr[0:1]
    low, high = jnp.minimum(first, second), jnp.maximum(first, second)
    gap = high - low
    kind = jnp.where(gap == 1, 0, jnp.where(gap == GV, 1, jnp.where(gap == GV + 1, 2, 3)))
    row_of = kind * GV + (low >> 4)
    col_of = low & (GV - 1)
    left = jnp.where(iota((64, E_PAD), 0) == row_of, strength, 0.0)
    lanes = iota((128, E_PAD), 0)
    right = ((lanes == col_of + 16) | (lanes == col_of + 80)).astype(F32)
    out_ref[...] = nt_dot(left, right)


def match_kernel(seam, count_ref, cand_s, cand_v, patch_ref, frame_ref, *rest):
    if seam == 0:
        other_ref, out_ref, a_scr, t_scr, s_scr = rest
    else:
        out_ref, a_scr, t_scr, s_scr = rest
    count = count_ref[seam]
    lane = iota((8, 128), 1)
    row = iota((8, 128), 0)

    def one_patch(p, carry):
        pixels = patch_ref[p].astype(F32)
        a_scr[...] = pixels
        a_sum = pixels[0:8]
        a_sq = pixels[0:8] * pixels[0:8]
        for t in range(1, 16):
            part = pixels[8 * t : 8 * t + 8]
            a_sum = a_sum + part
            a_sq = a_sq + part * part
        base = (seam * P_SIZE + p) * LINES
        for s in range(NS):
            move_y = cand_s[0, p * NS + s] + REACH
            move_x = cand_s[1, p * NS + s] + REACH
            odd = move_y & 1
            even_at = base + 3 * ((move_y + odd) >> 1)
            odd_at = base + 3 * ((move_y - odd) >> 1)
            even_late = lane < move_x
            odd_late = lane < move_x + 64
            odd_roll = (move_x + 64) & 127
            cross = jnp.zeros((8, 128), F32)
            total = jnp.zeros((8, 128), F32)
            square = jnp.zeros((8, 128), F32)
            for t in range(8):
                even_b = jnp.where(
                    even_late,
                    frame_ref[pl.ds(even_at + 24 * t + 1, 8, stride=3), :],
                    frame_ref[pl.ds(even_at + 24 * t, 8, stride=3), :],
                )
                odd_b = jnp.where(
                    odd_late,
                    frame_ref[pl.ds(odd_at + 24 * t + 2, 8, stride=3), :],
                    frame_ref[pl.ds(odd_at + 24 * t + 1, 8, stride=3), :],
                )
                even_a = pltpu.roll(a_scr[pl.ds(odd + 16 * t, 8, stride=2), :], move_x, 1)
                odd_a = pltpu.roll(a_scr[pl.ds(1 - odd + 16 * t, 8, stride=2), :], odd_roll, 1)
                cross = cross + even_a * even_b + odd_a * odd_b
                total = total + (even_b + odd_b)
                square = square + even_b * even_b + odd_b * odd_b
            t_scr[8 * s : 8 * s + 8, :] = cross
            t_scr[64 + 8 * s : 72 + 8 * s, :] = total
            t_scr[128 + 8 * s : 136 + 8 * s, :] = square
        spot = pl.multiple_of(p * 8, 8)
        for q in range(3):
            part = t_scr[pl.ds(64 * q, 8, stride=8), :]
            for k in range(1, 8):
                part = part + t_scr[pl.ds(64 * q + k, 8, stride=8), :]
            s_scr[pl.ds(q * 128 + spot, 8), :] = part
        for q, part in ((3, a_sum), (4, a_sq)):
            s_scr[pl.ds(q * 128 + spot, 8), :] = jnp.broadcast_to(
                jnp.sum(part, axis=0, keepdims=True), (8, 128)
            )
        return carry

    lax.fori_loop(0, count, one_patch, 0)
    ones = jnp.ones((8, 128), F32)
    cross, total, square, a_sum, a_sq = (
        nt_dot(ones, s_scr[128 * q : 128 * q + 128, :]) / PIXELS for q in range(5)
    )
    cov = cross - a_sum * total
    var_a = a_sq - a_sum * a_sum
    var_b = square - total * total
    ncc = cov / jnp.sqrt((var_a + EPSILON) * (var_b + EPSILON))
    weight = jnp.where((lane >> 3) < count, (1.5 + ncc) * (1.5 + ncc), 0.0)
    list_y = cand_v[0:1, :].astype(F32)
    list_x = cand_v[1:2, :].astype(F32)
    parts = jnp.where(
        row == 0,
        weight,
        jnp.where(row == 1, weight * list_y, jnp.where(row == 2, weight * list_x, 0.0)),
    )

    col = iota((128, 128), 1)
    slot_of = jnp.where(
        col < 16,
        col,
        jnp.where(col < 32, col - 16, jnp.where((col >= 80) & (col < 96), col - 80, -1)),
    )
    group = ((iota((128, 128), 0) >> 3) == slot_of).astype(F32)
    sums = jnp.dot(parts, group, precision=PRECISE, preferred_element_type=F32)
    w_sum, w_y, w_x = sums[0:1], sums[1:2], sums[2:3]
    slot = slot_of[0:1]
    alive = (slot >= 0) & (slot < count)
    conf = jnp.where(alive, w_sum / NS, 0.0)
    along_y = jnp.where(alive, w_y / (REACH * w_sum), 0.0)
    along_x = jnp.where(alive, w_x / (REACH * w_sum), 0.0)
    lane1 = lane[0:1]
    if seam == 1:
        q_row = jnp.where(lane1 < 16, 0.0, conf)
        f_row = q_row * jnp.where(lane1 < 64, along_y, along_x)
        out_ref[0:1, :] = q_row
        out_ref[1:2, :] = f_row
        out_ref[2:3, :] = along_y
        out_ref[3:4, :] = along_x
        out_ref[4:5, :] = conf
        out_ref[5:8, :] = jnp.zeros((3, 128), F32)
    else:
        gather = ((iota((16, 128), 1) >> 3) == iota((16, 128), 0)).astype(F32)
        cols = nt_dot(gather, parts)
        c_sum, c_y, c_x = cols[:, 0:1], cols[:, 1:2], cols[:, 2:3]
        alive_c = iota((16, 1), 0) < count
        conf_c = jnp.where(alive_c, c_sum / NS, 0.0)
        y_c = conf_c * jnp.where(alive_c, c_y / (REACH * c_sum), 0.0)
        x_c = conf_c * jnp.where(alive_c, c_x / (REACH * c_sum), 0.0)
        lane16 = iota((16, 128), 1)
        low, high = lane16 == 15, lane16 == 79
        out_ref[0:16, :] = jnp.where(low | high, conf_c, 0.0)
        out_ref[16:32, :] = jnp.where(low, y_c, jnp.where(high, x_c, 0.0))
        out_ref[32:40, :] = other_ref[...]
        out_ref[40:41, :] = along_y
        out_ref[41:42, :] = along_x
        out_ref[42:43, :] = conf
        out_ref[43:48, :] = jnp.zeros((5, 128), F32)


def krylov_kernel(pw_ref, pc_ref, pe_ref, ww_ref, wc_ref, we_ref, u_ref, mom_ref, match_ref):
    lane = iota((48, 128), 1)
    row = iota((48, 128), 0)

    def placed(west, centre, east):
        return pltpu.roll(west, 112, 1) + centre + pltpu.roll(east, 16, 1)

    def plane(t):
        rows = slice(16 * t, 16 * t + 16)
        stack = [
            jnp.concatenate([ref[a, rows, :] for a in range(3)], axis=0)
            for ref in (pw_ref, pc_ref, pe_ref)
        ]
        return placed(*stack)

    def west_seam(lo):
        centre = jnp.concatenate([wc_ref[a, lo : lo + 16, :] for a in range(3)], axis=0)
        east = jnp.concatenate([we_ref[a, lo : lo + 16, :] for a in range(3)], axis=0)
        return centre + pltpu.roll(east, 16, 1)

    def north_seam(r):
        out = jnp.zeros((48, 128), F32)
        for a in (1, 2):
            line = placed(*(ref[a, r : r + 1, :] for ref in (ww_ref, wc_ref, we_ref)))
            out = jnp.where(row == 16 * a - 1, line, out)
        return out

    q_h = plane(0) + west_seam(0)
    q_v = plane(1) + north_seam(32)
    q_d = plane(2)
    q_a = plane(3)
    f_h = west_seam(16)
    f_v = north_seam(33)

    def right(x):
        return pltpu.roll(x, 1, 1)

    def left(x):
        return pltpu.roll(x, 127, 1)

    def down(x):
        return pltpu.roll(x, 1, 0)

    def up(x):
        return pltpu.roll(x, 47, 0)

    def operate(v):
        below = up(v)
        h = q_h * (v - left(v))
        s = q_v * (v - below)
        d = q_d * (v - left(below))
        a = q_a * (v - right(below))
        out = (LAMBDA_REG - THETA) * v + (h + s) + (d + a)
        return out - right(h + down(d)) - down(s + left(a))

    u0 = f_h + f_v - right(f_h) - down(f_v)
    u1 = operate(u0)
    u2 = operate(u1)
    u3 = operate(u2)
    own = slice(16, 32)
    lane16 = lane[own]
    inside = ((lane16 >= 16) & (lane16 < 32)) | ((lane16 >= 80) & (lane16 < 96))
    parts = [jnp.where(inside, x[own], 0.0) for x in (u0, u1, u2, u3)]
    lane1 = iota((1, 128), 1)
    moments = jnp.zeros((1, 128), F32)
    for k in range(6):
        product = parts[k // 2] * parts[k // 2 + k % 2]
        value = jnp.sum(jnp.sum(product, axis=0, keepdims=True), axis=1, keepdims=True)
        moments = jnp.where(lane1 == k, value, moments)
    for k in range(3):
        u_ref[k] = parts[k]
    mom_ref[...] = jnp.broadcast_to(moments[None], mom_ref.shape)
    match_ref[0] = we_ref[1, 40:43, 0:16]
    match_ref[1] = wc_ref[2, 34:37, 0:16]


def combine_kernel(mom_ref, u_ref, out_ref):
    total = jnp.sum(mom_ref[...], axis=0)
    m = [total[:, k : k + 1] for k in range(6)]

    def gram(p, lift):
        out = None
        for i in range(3):
            for j in range(i, 3):
                if p[i] is None or p[j] is None:
                    continue
                term = m[i + j]
                if lift:
                    term = m[i + j + 1] + THETA * term
                term = (term * p[i]) * p[j]
                if j > i:
                    term = term + term
                out = term if out is None else out + term
        return out

    one = jnp.ones((1, 1), F32)
    r = [one, None, None]
    d = r
    rr = m[0]
    x = [None, None, None]

    def plus(a, b):
        return b if a is None else a if b is None else a + b

    def times(s, a):
        return None if a is None else s * a

    for step in range(3):
        alpha = rr / gram(d, True)
        x = [plus(x[i], times(alpha, d[i])) for i in range(3)]
        if step == 2:
            break
        image = [times(THETA, d[0]), plus(d[0], times(THETA, d[1])), plus(d[1], times(THETA, d[2]))]
        r = [plus(r[i], times(-alpha, image[i])) for i in range(3)]
        new = gram(r, False)
        d = [plus(r[i], times(new / rr, d[i])) for i in range(3)]
        rr = new
    field = x[0] * u_ref[0] + x[1] * u_ref[1] + x[2] * u_ref[2]
    vertex = iota((128, 256), 1)
    source = iota((128, 256), 0)
    keep = iota((16, 256), 0) == (iota((16, 256), 1) >> 4)
    for comp in range(2):
        spread = (source == (vertex & 15) + (16 + 64 * comp)).astype(F32)
        wide = jnp.dot(field, spread, precision=PRECISE, preferred_element_type=F32)
        out_ref[comp : comp + 1, :] = jnp.sum(jnp.where(keep, wide, 0.0), axis=0, keepdims=True)


def shape(dims, dtype=F32):
    return jax.ShapeDtypeStruct(dims, dtype)


def with_sides(x, axis):
    return shifted(x, axis, 1), shifted(x, axis, -1)


def body(patches, windows, candidates, live, edges, stiffness):
    tile_row = lax.axis_index("row")
    tile_col = lax.axis_index("col")
    west_patches = shifted(patches[0, 0, 0], "col", 1)
    north_patches = shifted(patches[0, 0, 1], "row", 1)
    west_cand = shifted(candidates[0, 0, 0], "col", 1)
    north_cand = shifted(candidates[0, 0, 1], "row", 1)
    count_west = jnp.where(tile_col > 0, live[tile_row, jnp.maximum(tile_col - 1, 0), 0], 0)
    count_north = jnp.where(tile_row > 0, live[jnp.maximum(tile_row - 1, 0), tile_col, 1], 0)
    counts = jnp.stack([count_west, count_north])

    frames = pl.pallas_call(
        frames_kernel,
        out_shape=shape((2 * P_SIZE * LINES, 128)),
        in_specs=[VMEM],
        out_specs=VMEM,
        compiler_params=pltpu.CompilerParams(vmem_limit_bytes=40 * 1024 * 1024),
    )(windows[0, 0])
    springs = pl.pallas_call(
        springs_kernel,
        out_shape=shape((64, 128)),
        in_specs=[VMEM, VMEM],
        out_specs=VMEM,
        scratch_shapes=[pltpu.VMEM((8, E_PAD), jnp.int32), pltpu.VMEM((8, E_PAD), F32)],
    )(edges[0], stiffness)
    north, south = with_sides(springs, "row")
    springs_c = jnp.stack([north, springs, south])
    springs_w, springs_e = with_sides(springs_c, "col")

    def match(seam, cand, raw, *other):
        return pl.pallas_call(
            functools.partial(match_kernel, seam),
            out_shape=shape((48 if seam == 0 else 8, 128)),
            in_specs=[SMEM, SMEM, VMEM, VMEM, VMEM] + [VMEM] * len(other),
            out_specs=VMEM,
            scratch_shapes=[
                pltpu.VMEM((128, 128), F32),
                pltpu.VMEM((192, 128), F32),
                pltpu.VMEM((640, 128), F32),
            ],
            compiler_params=pltpu.CompilerParams(vmem_limit_bytes=40 * 1024 * 1024),
        )(counts, cand, cand, raw, frames, *other)

    seam_north = match(1, north_cand, north_patches)
    seams = match(0, west_cand, west_patches, seam_north)
    north, south = with_sides(seams, "row")
    seams_c = jnp.stack([north, seams, south])
    seams_w, seams_e = with_sides(seams_c, "col")
    devices = lax.axis_size("row") * lax.axis_size("col")
    basis, moments, matches = pl.pallas_call(
        krylov_kernel,
        out_shape=(shape((3, 16, 128)), shape((devices, 1, 128)), shape((2, 3, P_SIZE))),
        in_specs=[VMEM] * 6,
        out_specs=(VMEM, VMEM, VMEM),
    )(springs_w, springs_c, springs_e, seams_w, seams_c, seams_e)
    moments = lax.all_to_all(moments, ("row", "col"), 0, 0)
    mesh_shift = pl.pallas_call(
        combine_kernel,
        out_shape=shape((2, GV * GV)),
        in_specs=[VMEM, VMEM],
        out_specs=VMEM,
    )(moments, basis)
    return matches[None, None], mesh_shift[None, None]


def solution(mesh):
    return jax.shard_map(
        body,
        mesh=mesh,
        in_specs=(
            P("row", "col", None, None, None, None),
            P("row", "col", None, None, None),
            P("row", "col", None, None, None),
            P(),
            P("row", None, "col"),
            P("row", "col"),
        ),
        out_specs=(P("row", "col", None, None, None), P("row", "col", None, None)),
        check_vma=False,
    )
```

```python
import functools

import jax
import jax.numpy as jnp
from jax import lax
from jax.experimental import pallas as pl
from jax.experimental.pallas import tpu as pltpu
from jax.sharding import PartitionSpec as P

PATCH = 128
REACH = 32
WIN = 192
NS = 8
P_SIZE = 16
GV = 16
E = 705
E_PAD = 768
LINES = WIN * WIN // 128
PIXELS = float(PATCH * PATCH)
LAMBDA_REG = 0.05
EPSILON = 1e-05
THETA = 8.0
PRECISE = lax.Precision.HIGHEST
F32 = jnp.float32
VMEM = pl.BlockSpec(memory_space=pltpu.VMEM)
SMEM = pl.BlockSpec(memory_space=pltpu.SMEM)


def shifted(x, axis, by):
    length = lax.axis_size(axis)
    pairs = [(i, i + by) for i in range(length) if 0 <= i + by < length]
    return lax.ppermute(x, axis, pairs)


def iota(shape, dim):
    return lax.broadcasted_iota(jnp.int32, shape, dim)


def nt_dot(a, b):
    return lax.dot_general(
        a, b, (((1,), (1,)), ((), ())), precision=PRECISE, preferred_element_type=F32
    )


def pack_kernel(patch_ref, cand_ref, east_ref, south_ref, sems):
    outs = (east_ref, south_ref)
    body_rows = P_SIZE * PATCH
    copies = [
        pltpu.make_async_copy(patch_ref.at[k], outs[k].at[pl.ds(0, body_rows)], sems.at[k])
        for k in range(2)
    ]
    for copy in copies:
        copy.start()
    for k in range(2):
        lists = jnp.concatenate([cand_ref[k].astype(F32), jnp.zeros((14, 128), F32)], axis=0)
        outs[k][body_rows : body_rows + 16, :] = lists.astype(jnp.bfloat16)
    for copy in copies:
        copy.wait()


def frames_kernel(win_ref, out_ref):
    for seam in range(2):

        def one_line(j, carry, seam=seam):
            at = pl.multiple_of(j * 128, 128)
            pixels = win_ref[seam, :, pl.ds(at, 128)].astype(F32)
            base = seam * P_SIZE * LINES + j
            out_ref[pl.ds(base, 8, stride=LINES), :] = pixels[:8]
            out_ref[pl.ds(base + 8 * LINES, 8, stride=LINES), :] = pixels[8:]
            return carry

        lax.fori_loop(0, LINES, one_line, 0, unroll=8)


def springs_kernel(edges_ref, stiff_ref, out_ref, ends_scr, stiff_scr):
    ends_scr[...] = jnp.zeros_like(ends_scr)
    stiff_scr[...] = jnp.zeros_like(stiff_scr)
    ends_scr[0:2, 0:E] = edges_ref[...]
    stiff_scr[0:1, 0:E] = stiff_ref[...]
    first, second = ends_scr[0:1], ends_scr[1:2]
    low, high = jnp.minimum(first, second), jnp.maximum(first, second)
    gap = high - low
    kind = jnp.where(gap == 1, 0, jnp.where(gap == GV, 1, jnp.where(gap == GV + 1, 2, 3)))
    left = jnp.where(iota((GV, E_PAD), 0) == (low >> 4), stiff_scr[0:1], 0.0)
    right = (iota((128, E_PAD), 0) == kind * GV + (low & (GV - 1))).astype(F32)
    out_ref[...] = nt_dot(left, right)


def match_kernel(seam, live_ref, sent_ref, frame_ref, *rest):
    if seam == 0:
        springs_ref, other_ref, out_ref, a_scr, t_scr, s_scr, list_scr, cand_s, sem = rest
    else:
        out_ref, a_scr, t_scr, s_scr, list_scr, cand_s, sem = rest
    lists = sent_ref[P_SIZE * PATCH : P_SIZE * PATCH + 16, :].astype(F32)
    list_scr[...] = lists[0:8].astype(jnp.int32)
    copy = pltpu.make_async_copy(list_scr, cand_s, sem)
    copy.start()
    copy.wait()
    tile_row, tile_col = lax.axis_index("row"), lax.axis_index("col")
    near_row, near_col = (tile_row, tile_col - 1) if seam == 0 else (tile_row - 1, tile_col)
    counts = live_ref[jnp.maximum(near_row, 0), seam : seam + 1, :]
    wanted = (iota((1, 16), 1) == near_col) & (near_row >= 0)
    count = jnp.sum(jnp.where(wanted, counts.astype(F32), 0.0), axis=1, keepdims=True)
    count = count.astype(jnp.int32)
    lane = iota((8, 128), 1)
    row = iota((8, 128), 0)

    def one_patch(p, carry):
        pixels = sent_ref[pl.ds(pl.multiple_of(p * PATCH, PATCH), PATCH), :].astype(F32)
        a_scr[...] = pixels
        a_sum = pixels[0:8]
        a_sq = pixels[0:8] * pixels[0:8]
        for t in range(1, 16):
            part = pixels[8 * t : 8 * t + 8]
            a_sum = a_sum + part
            a_sq = a_sq + part * part
        base = (seam * P_SIZE + p) * LINES
        for s in range(NS):
            move_y = cand_s[0, p * NS + s] + REACH
            move_x = cand_s[1, p * NS + s] + REACH
            odd = move_y & 1
            even_at = base + 3 * ((move_y + odd) >> 1)
            odd_at = base + 3 * ((move_y - odd) >> 1)
            even_late = lane < move_x
            odd_late = lane < move_x + 64
            odd_roll = (move_x + 64) & 127
            cross = jnp.zeros((8, 128), F32)
            total = jnp.zeros((8, 128), F32)
            square = jnp.zeros((8, 128), F32)
            for t in range(8):
                even_b = jnp.where(
                    even_late,
                    frame_ref[pl.ds(even_at + 24 * t + 1, 8, stride=3), :],
                    frame_ref[pl.ds(even_at + 24 * t, 8, stride=3), :],
                )
                odd_b = jnp.where(
                    odd_late,
                    frame_ref[pl.ds(odd_at + 24 * t + 2, 8, stride=3), :],
                    frame_ref[pl.ds(odd_at + 24 * t + 1, 8, stride=3), :],
                )
                even_a = pltpu.roll(a_scr[pl.ds(odd + 16 * t, 8, stride=2), :], move_x, 1)
                odd_a = pltpu.roll(a_scr[pl.ds(1 - odd + 16 * t, 8, stride=2), :], odd_roll, 1)
                cross = cross + even_a * even_b + odd_a * odd_b
                total = total + (even_b + odd_b)
                square = square + even_b * even_b + odd_b * odd_b
            t_scr[8 * s : 8 * s + 8, :] = cross
            t_scr[64 + 8 * s : 72 + 8 * s, :] = total
            t_scr[128 + 8 * s : 136 + 8 * s, :] = square
        spot = pl.multiple_of(p * 8, 8)
        for q in range(3):
            part = t_scr[pl.ds(64 * q, 8, stride=8), :]
            for k in range(1, 8):
                part = part + t_scr[pl.ds(64 * q + k, 8, stride=8), :]
            s_scr[pl.ds(q * 128 + spot, 8), :] = part
        for q, part in ((3, a_sum), (4, a_sq)):
            s_scr[pl.ds(q * 128 + spot, 8), :] = jnp.broadcast_to(
                jnp.sum(part, axis=0, keepdims=True), (8, 128)
            )
        return carry

    lax.fori_loop(0, P_SIZE, one_patch, 0)
    ones = jnp.ones((8, 128), F32)
    cross, total, square, a_sum, a_sq = (
        nt_dot(ones, s_scr[128 * q : 128 * q + 128, :]) / PIXELS for q in range(5)
    )
    cov = cross - a_sum * total
    var_a = a_sq - a_sum * a_sum
    var_b = square - total * total
    ncc = cov / jnp.sqrt((var_a + EPSILON) * (var_b + EPSILON))
    weight = jnp.where((lane >> 3) < count, (1.5 + ncc) * (1.5 + ncc), 0.0)
    parts = jnp.where(
        row == 0,
        weight,
        jnp.where(row == 1, weight * lists[0:1], jnp.where(row == 2, weight * lists[1:2], 0.0)),
    )
    group = ((iota((128, 128), 0) >> 3) == iota((128, 128), 1)).astype(F32)
    sums = jnp.dot(parts, group, precision=PRECISE, preferred_element_type=F32)

    def estimates(w_sum, w_y, w_x, slot):
        alive = slot < count
        conf = jnp.where(alive, w_sum / NS, 0.0)
        along_y = jnp.where(alive, w_y / (REACH * w_sum), 0.0)
        along_x = jnp.where(alive, w_x / (REACH * w_sum), 0.0)
        return conf, along_y, along_x

    conf, along_y, along_x = estimates(sums[0:1], sums[1:2], sums[2:3], lane[0:1])
    if seam == 1:
        lines = (conf, conf * along_y, conf * along_x, along_y, along_x)
        for k, line in enumerate(lines):
            out_ref[k : k + 1, :] = line
        out_ref[5:8, :] = jnp.zeros((3, 128), F32)
    else:
        gather = ((iota((16, 128), 1) >> 3) == iota((16, 128), 0)).astype(F32)
        cols = nt_dot(gather, parts)
        conf_c, y_c, x_c = estimates(cols[:, 0:1], cols[:, 1:2], cols[:, 2:3], iota((16, 1), 0))
        lane16 = iota((16, 128), 1)
        block = springs_ref[...]
        for k, col in enumerate((conf_c, conf_c * y_c, conf_c * x_c)):
            block = jnp.where(lane16 == 64 + k, col, block)
        out_ref[0:16, :] = block
        out_ref[16:24, :] = other_ref[...]
        for k, line in enumerate((along_y, along_x, conf)):
            out_ref[21 + k : 22 + k, :] = line


def krylov_kernel(west_ref, centre_ref, east_ref, u_ref, mom_ref, match_ref):
    lane = iota((48, 128), 1)
    row = iota((48, 128), 0)
    refs = (west_ref, centre_ref, east_ref)
    blocks = [jnp.concatenate([ref[a, 0:16, :] for a in range(3)], axis=0) for ref in refs]

    def both(x):
        return x + pltpu.roll(x, 64, 1)

    def plane(t):
        out = jnp.zeros((48, 128), F32)
        for b in range(3):
            moved = pltpu.roll(blocks[b], (16 * b - 16 * t) % 128, 1)
            out = jnp.where((lane >> 4) == b, moved, out)
        return both(out)

    def west_seam(lane_y, lane_x):
        out = jnp.zeros((48, 128), F32)
        for b in (1, 2):
            out = jnp.where(lane == 16 * b - 1, blocks[b][:, lane_y : lane_y + 1], out)
            out = jnp.where(lane == 16 * b + 63, blocks[b][:, lane_x : lane_x + 1], out)
        return out

    def north_lines(a, r):
        lines = [ref[a, r : r + 1, :] for ref in refs]
        return lines[0] + pltpu.roll(lines[1], 16, 1) + pltpu.roll(lines[2], 32, 1)

    def north_seam(r_y, r_x):
        out = jnp.zeros((48, 128), F32)
        for a in (1, 2):
            line = north_lines(a, r_y) + pltpu.roll(north_lines(a, r_x), 64, 1)
            out = jnp.where(row == 16 * a - 1, line, out)
        return out

    q_h = plane(0) + west_seam(64, 64)
    q_v = plane(1) + north_seam(16, 16)
    q_d = plane(2)
    q_a = plane(3)
    f_h = west_seam(65, 66)
    f_v = north_seam(17, 18)

    def right(x):
        return pltpu.roll(x, 1, 1)

    def left(x):
        return pltpu.roll(x, 127, 1)

    def down(x):
        return pltpu.roll(x, 1, 0)

    def up(x):
        return pltpu.roll(x, 47, 0)

    def operate(v):
        below = up(v)
        h = q_h * (v - left(v))
        s = q_v * (v - below)
        d = q_d * (v - left(below))
        a = q_a * (v - right(below))
        out = (LAMBDA_REG - THETA) * v + (h + s) + (d + a)
        return out - right(h + down(d)) - down(s + left(a))

    u0 = f_h + f_v - right(f_h) - down(f_v)
    u1 = operate(u0)
    u2 = operate(u1)
    u3 = operate(u2)
    own = slice(16, 32)
    lane16 = lane[own]
    inside = ((lane16 >= 16) & (lane16 < 32)) | ((lane16 >= 80) & (lane16 < 96))
    parts = [jnp.where(inside, x[own], 0.0) for x in (u0, u1, u2, u3)]
    lane1 = iota((1, 128), 1)
    moments = jnp.zeros((1, 128), F32)
    for k in range(6):
        product = parts[k // 2] * parts[k // 2 + k % 2]
        value = jnp.sum(jnp.sum(product, axis=0, keepdims=True), axis=1, keepdims=True)
        moments = jnp.where(lane1 == k, value, moments)
    for k in range(3):
        u_ref[k] = parts[k]
    mom_ref[...] = jnp.broadcast_to(moments[None], mom_ref.shape)
    for k, (east_row, south_row) in enumerate(((21, 19), (22, 20), (23, 16))):
        match_ref[k, 0:1, :] = east_ref[1, east_row : east_row + 1, 0:16]
        match_ref[k, 1:2, :] = centre_ref[2, south_row : south_row + 1, 0:16]


def flatten_kernel(u_ref, out_ref):
    vertex = iota((128, 256), 1)
    source = iota((128, 256), 0)
    fields = jnp.concatenate([u_ref[k] for k in range(3)], axis=0)
    keep = iota((16, 256), 0) == (iota((16, 256), 1) >> 4)
    for comp in range(2):
        spread = (source == (vertex & 15) + (16 + 64 * comp)).astype(F32)
        wide = jnp.dot(fields, spread, precision=PRECISE, preferred_element_type=F32)
        for k in range(3):
            line = jnp.where(keep, wide[16 * k : 16 * k + 16], 0.0)
            out_ref[k, comp : comp + 1, :] = jnp.sum(line, axis=0, keepdims=True)


def combine_kernel(mom_ref, u_ref, out_ref):
    total = jnp.sum(mom_ref[...], axis=0, keepdims=True)
    m = [total[:, k : k + 1] for k in range(6)]

    def gram(p, lift):
        out = None
        for i in range(3):
            for j in range(i, 3):
                if p[i] is None or p[j] is None:
                    continue
                term = m[i + j]
                if lift:
                    term = m[i + j + 1] + THETA * term
                term = (term * p[i]) * p[j]
                if j > i:
                    term = term + term
                out = term if out is None else out + term
        return out

    one = jnp.ones((1, 1), F32)
    r = [one, None, None]
    d = r
    rr = m[0]
    x = [None, None, None]

    def plus(a, b):
        return b if a is None else a if b is None else a + b

    def times(s, a):
        return None if a is None else s * a

    for step in range(3):
        alpha = rr / gram(d, True)
        x = [plus(x[i], times(alpha, d[i])) for i in range(3)]
        if step == 2:
            break
        image = [times(THETA, d[0]), plus(d[0], times(THETA, d[1])), plus(d[1], times(THETA, d[2]))]
        r = [plus(r[i], times(-alpha, image[i])) for i in range(3)]
        new = gram(r, False)
        d = [plus(r[i], times(new / rr, d[i])) for i in range(3)]
        rr = new
    out_ref[...] = x[0] * u_ref[0] + x[1] * u_ref[1] + x[2] * u_ref[2]


def limit(mib):
    return pltpu.CompilerParams(vmem_limit_bytes=mib * 1024 * 1024)


def shape(dims, dtype=F32):
    return jax.ShapeDtypeStruct(dims, dtype)


def with_sides(x, axis):
    return shifted(x, axis, 1), shifted(x, axis, -1)


def call_frames(windows):
    return pl.pallas_call(
        frames_kernel,
        out_shape=shape((2 * P_SIZE * LINES, 128)),
        in_specs=[VMEM],
        out_specs=VMEM,
        compiler_params=limit(10),
    )(windows)


def call_match(seam, *operands):
    return pl.pallas_call(
        functools.partial(match_kernel, seam),
        out_shape=shape((24 if seam == 0 else 8, 128)),
        in_specs=[VMEM] * len(operands),
        out_specs=VMEM,
        scratch_shapes=[
            pltpu.VMEM((128, 128), F32),
            pltpu.VMEM((192, 128), F32),
            pltpu.VMEM((640, 128), F32),
            pltpu.VMEM((8, 128), jnp.int32),
            pltpu.SMEM((8, 128), jnp.int32),
            pltpu.SemaphoreType.DMA,
        ],
        compiler_params=limit(10),
    )(*operands)


def body(patches, windows, candidates, live, edges, stiffness):
    to_east, to_south = pl.pallas_call(
        pack_kernel,
        out_shape=(shape((P_SIZE * PATCH + 16, 128), jnp.bfloat16),) * 2,
        in_specs=[pl.BlockSpec(memory_space=pl.ANY), VMEM],
        out_specs=(VMEM, VMEM),
        scratch_shapes=[pltpu.SemaphoreType.DMA((2,))],
        compiler_params=limit(4),
    )(patches.reshape(2, P_SIZE * PATCH, PATCH), candidates[0, 0])
    sent_west = shifted(to_east, "col", 1)
    sent_north = shifted(to_south, "row", 1)
    live = live.transpose(0, 2, 1)

    frames = call_frames(windows[0, 0])
    springs = pl.pallas_call(
        springs_kernel,
        out_shape=shape((GV, 128)),
        in_specs=[VMEM, VMEM],
        out_specs=VMEM,
        scratch_shapes=[pltpu.VMEM((8, E_PAD), jnp.int32), pltpu.VMEM((8, E_PAD), F32)],
        compiler_params=limit(4),
    )(edges[0], stiffness)
    seam_north = call_match(1, live, sent_north, frames)
    own = call_match(0, live, sent_west, frames, springs, seam_north)
    north, south = with_sides(own, "row")
    centre = jnp.stack([north, own, south])
    west, east = with_sides(centre, "col")
    devices = lax.axis_size("row") * lax.axis_size("col")
    basis, moments, matches = pl.pallas_call(
        krylov_kernel,
        out_shape=(shape((3, 16, 128)), shape((devices, 1, 128)), shape((3, 2, P_SIZE))),
        in_specs=[VMEM] * 3,
        out_specs=(VMEM, VMEM, VMEM),
        compiler_params=limit(4),
    )(west, centre, east)
    moments = lax.all_to_all(moments, ("row", "col"), 0, 0).reshape(devices, 128)
    flat = pl.pallas_call(
        flatten_kernel,
        out_shape=shape((3, 2, GV * GV)),
        in_specs=[VMEM],
        out_specs=VMEM,
        compiler_params=limit(4),
    )(basis)
    mesh_shift = pl.pallas_call(
        combine_kernel,
        out_shape=shape((2, GV * GV)),
        in_specs=[VMEM, VMEM],
        out_specs=VMEM,
        compiler_params=limit(4),
    )(moments, flat)
    return matches.transpose(1, 0, 2)[None, None], mesh_shift[None, None]


def solution(mesh):
    return jax.shard_map(
        body,
        mesh=mesh,
        in_specs=(
            P("row", "col", None, None, None, None),
            P("row", "col", None, None, None),
            P("row", "col", None, None, None),
            P(),
            P("row", None, "col"),
            P("row", "col"),
        ),
        out_specs=(P("row", "col", None, None, None), P("row", "col", None, None)),
        check_vma=False,
    )
```

```python
import functools

import jax
import jax.numpy as jnp
from jax import lax
from jax.experimental import pallas as pl
from jax.experimental.pallas import tpu as pltpu
from jax.sharding import PartitionSpec as P

PATCH = 128
REACH = 32
WIN = 192
NS = 8
P_SIZE = 16
P_EARLY = 8
GV = 16
E = 705
E_PAD = 768
PITCH = 2 * WIN + 1
PIXELS = float(PATCH * PATCH)
LAMBDA_REG = 0.05
EPSILON = 1e-05
THETA = 8.0
PRECISE = lax.Precision.HIGHEST
F32 = jnp.float32
VMEM = pl.BlockSpec(memory_space=pltpu.VMEM)
HBM = pl.BlockSpec(memory_space=pltpu.HBM)


def shifted(x, axis, by):
    length = lax.axis_size(axis)
    pairs = [(i, i + by) for i in range(length) if 0 <= i + by < length]
    return lax.ppermute(x, axis, pairs)


def iota(shape, dim):
    return lax.broadcasted_iota(jnp.int32, shape, dim)


def nt_dot(a, b):
    return lax.dot_general(
        a, b, (((1,), (1,)), ((), ())), precision=PRECISE, preferred_element_type=F32
    )


def pack_kernel(patch_ref, cand_ref, first_ref, south_ref, second_ref, sems):
    moves = ((0, 0, first_ref), (1, 0, south_ref), (0, P_EARLY, second_ref))
    copies = []
    for k, (seam, slot, out_ref) in enumerate(moves):
        rows = out_ref.shape[0] // PATCH * PATCH
        copies.append(
            pltpu.make_async_copy(
                patch_ref.at[seam, pl.ds(slot * PATCH, rows)],
                out_ref.at[pl.ds(0, rows)],
                sems.at[k],
            )
        )
        copies[-1].start()
    for seam, out_ref in ((0, first_ref), (1, south_ref)):
        rows = out_ref.shape[0] // PATCH * PATCH
        tile = jnp.concatenate([cand_ref[seam].astype(F32), jnp.zeros((14, 128), F32)], axis=0)
        out_ref[rows : rows + 16, :] = tile.astype(jnp.bfloat16)
    for copy in copies:
        copy.wait()


def frames_kernel(win_ref, out_ref):
    low = iota((P_SIZE, 128), 1) < 64
    for seam in range(2):

        def one_pair(m, carry, seam=seam):
            line = [
                win_ref[seam, :, pl.ds(pl.multiple_of(m * 384 + c * 128, 128), 128)].astype(F32)
                for c in range(3)
            ]
            last = pltpu.roll(line[2], 64, 1)
            middle = jnp.where(low, pltpu.roll(line[1], 64, 1), last)
            spot = seam * P_SIZE * PITCH + 2 * m
            for shift, value in ((0, line[0]), (1, middle), (WIN, line[1]), (WIN + 1, last)):
                for half in range(2):
                    at = spot + half * 8 * PITCH + shift
                    out_ref[pl.ds(at, 8, stride=PITCH), :] = value[8 * half : 8 * half + 8]
            return carry

        lax.fori_loop(0, WIN // 2, one_pair, 0, unroll=32)


def springs_kernel(edges_ref, stiff_ref, out_ref, ends_scr, stiff_scr):
    ends_scr[...] = jnp.zeros_like(ends_scr)
    stiff_scr[...] = jnp.zeros_like(stiff_scr)
    ends_scr[0:2, 0:E] = edges_ref[...]
    stiff_scr[0:1, 0:E] = stiff_ref[...]
    first, second = ends_scr[0:1], ends_scr[1:2]
    low, high = jnp.minimum(first, second), jnp.maximum(first, second)
    gap = high - low
    kind = jnp.where(gap == 1, 0, jnp.where(gap == GV, 1, jnp.where(gap == GV + 1, 2, 3)))
    left = jnp.where(iota((GV, E_PAD), 0) == (low >> 4), stiff_scr[0:1], 0.0)
    right = (iota((128, E_PAD), 0) == kind * GV + (low & (GV - 1))).astype(F32)
    out_ref[...] = nt_dot(left, right)


def split3(x):
    first = x.astype(jnp.bfloat16)
    rest = x - first.astype(F32)
    second = rest.astype(jnp.bfloat16)
    third = (rest - second.astype(F32)).astype(jnp.bfloat16)
    return first, second, third


def fold(x):
    pieces = [x[8 * t : 8 * t + 8] for t in range(x.shape[0] // 8)]
    while len(pieces) > 1:
        pieces = [a + b for a, b in zip(pieces[::2], pieces[1::2])]
    return pieces[0]


def score(seam, first, slots, tail_ref, sent_ref, frame_ref, s_ref, at, scratch):
    a_scr, t_scr, list_scr, cand_s, sem = scratch
    rows = s_ref.shape[0] // 5
    tail = tail_ref.shape[0] // PATCH * PATCH
    lists = tail_ref[tail : tail + 16, :].astype(F32)
    list_scr[...] = lists[0:8].astype(jnp.int32)
    copy = pltpu.make_async_copy(list_scr, cand_s, sem)
    copy.start()
    full_lane = iota((PATCH, 128), 1)

    def one_sum(p, carry):
        pixels = sent_ref[pl.ds(pl.multiple_of(p * PATCH, PATCH), PATCH), :].astype(F32)
        spot = pl.multiple_of(at + p * 8, 8)
        for q, part in ((3, fold(pixels)), (4, fold(pixels * pixels))):
            s_ref[pl.ds(q * rows + spot, 8), :] = jnp.broadcast_to(
                jnp.sum(part, axis=0, keepdims=True), (8, 128)
            )
        return carry

    lax.fori_loop(0, slots, one_sum, 0, unroll=2)
    copy.wait()

    def one_patch(p, carry):
        pixels = sent_ref[pl.ds(pl.multiple_of(p * PATCH, PATCH), PATCH), :]
        a_scr[...] = pixels.astype(F32)
        base = (seam * P_SIZE + first + p) * PITCH
        for s in range(NS):
            top = base + (cand_s[0, (first + p) * NS + s] + REACH)
            move_x = cand_s[1, (first + p) * NS + s] + REACH
            crop = jnp.where(
                full_lane < move_x,
                frame_ref[pl.ds(top + WIN, PATCH), :],
                frame_ref[pl.ds(top, PATCH), :],
            )
            cross = fold(pltpu.roll(a_scr[...], move_x, 1) * crop)
            total = fold(crop)
            square = fold(crop * crop)
            for q, part in enumerate((cross, total, square)):
                t_scr[72 * q + 9 * s : 72 * q + 9 * s + 8, :] = part
        spot = pl.multiple_of(at + p * 8, 8)
        for q in range(3):
            part = t_scr[pl.ds(72 * q, 8, stride=9), :]
            for k in range(1, 8):
                part = part + t_scr[pl.ds(72 * q + k, 8, stride=9), :]
            s_ref[pl.ds(q * rows + spot, 8), :] = part
        return carry

    lax.fori_loop(0, slots, one_patch, 0, unroll=2)
    return lists


def early_kernel(tail_ref, frame_ref, s_ref, *scratch):
    score(0, 0, P_EARLY, tail_ref, tail_ref, frame_ref, s_ref, 0, scratch)


def match_kernel(seam, live_ref, tail_ref, frame_ref, *rest):
    if seam == 0:
        sent_ref, early_ref, springs_ref, other_ref, out_ref, s_scr = rest[:6]
        done = P_EARLY * NS
        for q in range(5):
            s_scr[128 * q : 128 * q + done, :] = early_ref[done * q : done * q + done, :]
        lists = score(
            0, P_EARLY, P_SIZE - P_EARLY, tail_ref, sent_ref, frame_ref, s_scr, done, rest[6:]
        )
    else:
        out_ref, s_scr = rest[:2]
        lists = score(1, 0, P_SIZE, tail_ref, tail_ref, frame_ref, s_scr, 0, rest[2:])
    tile_row, tile_col = lax.axis_index("row"), lax.axis_index("col")
    near_row, near_col = (tile_row, tile_col - 1) if seam == 0 else (tile_row - 1, tile_col)
    counts = live_ref[jnp.maximum(near_row, 0), seam : seam + 1, :]
    wanted = (iota((1, 16), 1) == near_col) & (near_row >= 0)
    count = jnp.sum(jnp.where(wanted, counts.astype(F32), 0.0), axis=1, keepdims=True)
    count = count.astype(jnp.int32)
    lane = iota((8, 128), 1)
    row = iota((8, 128), 0)
    cross, total, square, a_sum, a_sq = (
        jnp.sum(s_scr[128 * q : 128 * q + 128, :].T, axis=0, keepdims=True) / PIXELS
        for q in range(5)
    )
    cov = cross - a_sum * total
    var_a = a_sq - a_sum * a_sum
    var_b = square - total * total
    ncc = cov / jnp.sqrt((var_a + EPSILON) * (var_b + EPSILON))
    weight = jnp.where((lane[0:1] >> 3) < count, (1.5 + ncc) * (1.5 + ncc), 0.0)
    parts = jnp.where(
        row == 0,
        weight,
        jnp.where(row == 1, weight * lists[0:1], jnp.where(row == 2, weight * lists[1:2], 0.0)),
    )
    group = ((iota((128, 128), 0) >> 3) == iota((128, 128), 1)).astype(jnp.bfloat16)
    sums = [jnp.dot(part, group, preferred_element_type=F32) for part in split3(parts)]
    sums = sums[0] + sums[1] + sums[2]

    def estimates(w_sum, w_y, w_x, slot):
        alive = slot < count
        conf = jnp.where(alive, w_sum / NS, 0.0)
        along_y = jnp.where(alive, w_y / (REACH * w_sum), 0.0)
        along_x = jnp.where(alive, w_x / (REACH * w_sum), 0.0)
        return conf, along_y, along_x

    conf, along_y, along_x = estimates(sums[0:1], sums[1:2], sums[2:3], lane[0:1])
    if seam == 1:
        lines = (conf, conf * along_y, conf * along_x, along_y, along_x)
        for k, line in enumerate(lines):
            out_ref[k : k + 1, :] = line
        out_ref[5:8, :] = jnp.zeros((3, 128), F32)
    else:
        lines = (conf, conf * along_y, conf * along_x)
        cols = jnp.concatenate(lines + (jnp.zeros((5, 128), F32),), axis=0).T
        lane16 = iota((16, 128), 1)
        block = springs_ref[...]
        for k in range(3):
            block = jnp.where(lane16 == 64 + k, cols[0:16, k : k + 1], block)
        out_ref[0:16, :] = block
        out_ref[16:24, :] = other_ref[...]
        for k, line in enumerate((along_y, along_x, conf)):
            out_ref[21 + k : 22 + k, :] = line


def krylov_kernel(inner_ref, centre_ref, outer_ref, u_ref, mom_ref, match_ref):
    odd = lax.axis_index("col") % 2 == 1
    west = jnp.where(odd, inner_ref[...], outer_ref[...])
    east = jnp.where(odd, outer_ref[...], inner_ref[...])
    tiles = (west, centre_ref[...], east)
    lane = iota((48, 128), 1)
    row = iota((48, 128), 0)
    blocks = [jnp.concatenate([tile[a, 0:16, :] for a in range(3)], axis=0) for tile in tiles]

    def both(x):
        return x + pltpu.roll(x, 64, 1)

    def plane(t):
        out = jnp.zeros((48, 128), F32)
        for b in range(3):
            moved = pltpu.roll(blocks[b], (16 * b - 16 * t) % 128, 1)
            out = jnp.where((lane >> 4) == b, moved, out)
        return both(out)

    def west_seam(lane_y, lane_x):
        out = jnp.zeros((48, 128), F32)
        for b in (1, 2):
            out = jnp.where(lane == 16 * b - 1, blocks[b][:, lane_y : lane_y + 1], out)
            out = jnp.where(lane == 16 * b + 63, blocks[b][:, lane_x : lane_x + 1], out)
        return out

    def north_lines(a, r):
        lines = [tile[a, r : r + 1, :] for tile in tiles]
        return lines[0] + pltpu.roll(lines[1], 16, 1) + pltpu.roll(lines[2], 32, 1)

    def north_seam(r_y, r_x):
        out = jnp.zeros((48, 128), F32)
        for a in (1, 2):
            line = north_lines(a, r_y) + pltpu.roll(north_lines(a, r_x), 64, 1)
            out = jnp.where(row == 16 * a - 1, line, out)
        return out

    q_h = plane(0) + west_seam(64, 64)
    q_v = plane(1) + north_seam(16, 16)
    q_d = plane(2)
    q_a = plane(3)
    f_h = west_seam(65, 66)
    f_v = north_seam(17, 18)

    def right(x):
        return pltpu.roll(x, 1, 1)

    def left(x):
        return pltpu.roll(x, 127, 1)

    def down(x):
        return pltpu.roll(x, 1, 0)

    def up(x):
        return pltpu.roll(x, 47, 0)

    def operate(v):
        below = up(v)
        h = q_h * (v - left(v))
        s = q_v * (v - below)
        d = q_d * (v - left(below))
        a = q_a * (v - right(below))
        out = (LAMBDA_REG - THETA) * v + (h + s) + (d + a)
        return out - right(h + down(d)) - down(s + left(a))

    u0 = f_h + f_v - right(f_h) - down(f_v)
    u1 = operate(u0)
    u2 = operate(u1)
    u3 = operate(u2)
    own = slice(16, 32)
    lane16 = lane[own]
    inside = ((lane16 >= 16) & (lane16 < 32)) | ((lane16 >= 80) & (lane16 < 96))
    parts = [jnp.where(inside, x[own], 0.0) for x in (u0, u1, u2, u3)]
    lane1 = iota((1, 128), 1)
    moments = jnp.zeros((1, 128), F32)
    for k in range(6):
        product = parts[k // 2] * parts[k // 2 + k % 2]
        value = jnp.sum(jnp.sum(product, axis=0, keepdims=True), axis=1, keepdims=True)
        moments = jnp.where(lane1 == k, value, moments)
    for k in range(3):
        u_ref[k] = parts[k]
    mom_ref[...] = jnp.broadcast_to(moments[None], mom_ref.shape)
    for k, (east_row, south_row) in enumerate(((21, 19), (22, 20), (23, 16))):
        match_ref[k, 0:1, :] = east[1, east_row : east_row + 1, 0:16]
        match_ref[k, 1:2, :] = centre_ref[2, south_row : south_row + 1, 0:16]


def flatten_kernel(u_ref, out_ref):
    vertex = iota((128, 256), 1)
    source = iota((128, 256), 0)
    fields = jnp.concatenate([u_ref[k] for k in range(3)], axis=0)
    keep = iota((16, 256), 0) == (iota((16, 256), 1) >> 4)
    for comp in range(2):
        spread = (source == (vertex & 15) + (16 + 64 * comp)).astype(F32)
        wide = jnp.dot(fields, spread, precision=PRECISE, preferred_element_type=F32)
        for k in range(3):
            line = jnp.where(keep, wide[16 * k : 16 * k + 16], 0.0)
            out_ref[k, comp : comp + 1, :] = jnp.sum(line, axis=0, keepdims=True)


def combine_kernel(mom_ref, u_ref, out_ref):
    total = jnp.sum(mom_ref[...], axis=0, keepdims=True)
    m = [total[:, k : k + 1] for k in range(6)]

    def gram(p, lift):
        out = None
        for i in range(3):
            for j in range(i, 3):
                if p[i] is None or p[j] is None:
                    continue
                term = m[i + j]
                if lift:
                    term = m[i + j + 1] + THETA * term
                term = (term * p[i]) * p[j]
                if j > i:
                    term = term + term
                out = term if out is None else out + term
        return out

    one = jnp.ones((1, 1), F32)
    r = [one, None, None]
    d = r
    rr = m[0]
    x = [None, None, None]

    def plus(a, b):
        return b if a is None else a if b is None else a + b

    def times(s, a):
        return None if a is None else s * a

    for step in range(3):
        alpha = rr / gram(d, True)
        x = [plus(x[i], times(alpha, d[i])) for i in range(3)]
        if step == 2:
            break
        image = [times(THETA, d[0]), plus(d[0], times(THETA, d[1])), plus(d[1], times(THETA, d[2]))]
        r = [plus(r[i], times(-alpha, image[i])) for i in range(3)]
        new = gram(r, False)
        d = [plus(r[i], times(new / rr, d[i])) for i in range(3)]
        rr = new
    out_ref[...] = x[0] * u_ref[0] + x[1] * u_ref[1] + x[2] * u_ref[2]


def limit(mib):
    return pltpu.CompilerParams(vmem_limit_bytes=mib * 1024 * 1024)


def shape(dims, dtype=F32):
    return jax.ShapeDtypeStruct(dims, dtype)


def swaps(x, axis):
    length = lax.axis_size(axis)
    inner = [(i, i ^ 1) for i in range(length)]
    outer = [(i, i + 1 if i % 2 else i - 1) for i in range(1, length - 1)]
    return lax.ppermute(x, axis, inner), lax.ppermute(x, axis, outer)


def call_pack(patches, candidates):
    return pl.pallas_call(
        pack_kernel,
        out_shape=tuple(
            shape((rows, 128), jnp.bfloat16)
            for rows in (P_EARLY * PATCH + 16, P_SIZE * PATCH + 16, (P_SIZE - P_EARLY) * PATCH)
        ),
        in_specs=[HBM, VMEM],
        out_specs=(VMEM, VMEM, VMEM),
        scratch_shapes=[pltpu.SemaphoreType.DMA((3,))],
        compiler_params=limit(4),
    )(patches, candidates)


def call_frames(windows):
    return pl.pallas_call(
        frames_kernel,
        out_shape=shape((2 * P_SIZE * PITCH, 128)),
        in_specs=[VMEM],
        out_specs=VMEM,
        compiler_params=limit(12),
    )(windows)


def score_scratch():
    return [
        pltpu.VMEM((128, 128), F32),
        pltpu.VMEM((216, 128), F32),
        pltpu.VMEM((8, 128), jnp.int32),
        pltpu.SMEM((8, 128), jnp.int32),
        pltpu.SemaphoreType.DMA,
    ]


def call_early(*operands):
    return pl.pallas_call(
        early_kernel,
        out_shape=shape((5 * P_EARLY * NS, 128)),
        in_specs=[VMEM] * len(operands),
        out_specs=VMEM,
        scratch_shapes=score_scratch(),
        compiler_params=limit(12),
    )(*operands)


def call_match(seam, *operands):
    return pl.pallas_call(
        functools.partial(match_kernel, seam),
        out_shape=shape((24 if seam == 0 else 8, 128)),
        in_specs=[VMEM] * len(operands),
        out_specs=VMEM,
        scratch_shapes=[pltpu.VMEM((5 * P_SIZE * NS, 128), F32)] + score_scratch(),
        compiler_params=limit(12),
    )(*operands)


def body(patches, windows, candidates, live, edges, stiffness):
    first, to_south, second = call_pack(
        patches.reshape(2, P_SIZE * PATCH, PATCH), candidates[0, 0]
    )
    west_first = shifted(first, "col", 1)
    sent_north = shifted(to_south, "row", 1)
    west_second = shifted(second, "col", 1)
    live = live.transpose(0, 2, 1)

    frames = call_frames(windows[0, 0])
    springs = pl.pallas_call(
        springs_kernel,
        out_shape=shape((GV, 128)),
        in_specs=[VMEM, VMEM],
        out_specs=VMEM,
        scratch_shapes=[pltpu.VMEM((8, E_PAD), jnp.int32), pltpu.VMEM((8, E_PAD), F32)],
        compiler_params=limit(4),
    )(edges[0], stiffness)
    early = call_early(west_first, frames)
    seam_north = call_match(1, live, sent_north, frames)
    own = call_match(0, live, west_first, frames, west_second, early, springs, seam_north)
    inner, outer = swaps(own, "row")
    odd = lax.axis_index("row") % 2 == 1
    centre = jnp.stack([jnp.where(odd, inner, outer), own, jnp.where(odd, outer, inner)])
    inner, outer = swaps(centre, "col")
    devices = lax.axis_size("row") * lax.axis_size("col")
    basis, moments, matches = pl.pallas_call(
        krylov_kernel,
        out_shape=(shape((3, 16, 128)), shape((devices, 1, 128)), shape((3, 2, P_SIZE))),
        in_specs=[VMEM] * 3,
        out_specs=(VMEM, VMEM, VMEM),
        compiler_params=limit(4),
    )(inner, centre, outer)
    moments = lax.all_to_all(moments, ("row", "col"), 0, 0).reshape(devices, 128)
    flat = pl.pallas_call(
        flatten_kernel,
        out_shape=shape((3, 2, GV * GV)),
        in_specs=[VMEM],
        out_specs=VMEM,
        compiler_params=limit(4),
    )(basis)
    mesh_shift = pl.pallas_call(
        combine_kernel,
        out_shape=shape((2, GV * GV)),
        in_specs=[VMEM, VMEM],
        out_specs=VMEM,
        compiler_params=limit(4),
    )(moments, flat)
    return matches.transpose(1, 0, 2)[None, None], mesh_shift[None, None]


def solution(mesh):
    return jax.shard_map(
        body,
        mesh=mesh,
        in_specs=(
            P("row", "col", None, None, None, None),
            P("row", "col", None, None, None),
            P("row", "col", None, None, None),
            P(),
            P("row", None, "col"),
            P("row", "col"),
        ),
        out_specs=(P("row", "col", None, None, None), P("row", "col", None, None)),
        check_vma=False,
    )
```

```python
import functools

import jax
import jax.numpy as jnp
from jax import lax
from jax.experimental import pallas as pl
from jax.experimental.pallas import tpu as pltpu
from jax.sharding import PartitionSpec as P

PATCH = 128
REACH = 32
WIN = 192
NS = 8
P_SIZE = 16
GV = 16
E = 705
E_PAD = 768
PITCH = 2 * WIN + 1
TOPS = WIN - PATCH + 1
TAB = 4 * TOPS + 1
PIXELS = float(PATCH * PATCH)
LAMBDA_REG = 0.05
EPSILON = 1e-05
THETA = 8.0
PRECISE = lax.Precision.HIGHEST
F32 = jnp.float32
VMEM = pl.BlockSpec(memory_space=pltpu.VMEM)
HBM = pl.BlockSpec(memory_space=pltpu.HBM)


def shifted(x, axis, by):
    length = lax.axis_size(axis)
    pairs = [(i, i + by) for i in range(length) if 0 <= i + by < length]
    return lax.ppermute(x, axis, pairs)


def iota(shape, dim):
    return lax.broadcasted_iota(jnp.int32, shape, dim)


def nt_dot(a, b):
    return lax.dot_general(
        a, b, (((1,), (1,)), ((), ())), precision=PRECISE, preferred_element_type=F32
    )


def pack_kernel(patch_ref, cand_ref, east_ref, south_ref, sems):
    outs = (east_ref, south_ref)
    body_rows = P_SIZE * PATCH
    copies = [
        pltpu.make_async_copy(patch_ref.at[k], outs[k].at[pl.ds(0, body_rows)], sems.at[k])
        for k in range(2)
    ]
    for copy in copies:
        copy.start()
    for k in range(2):
        tail = outs[k].shape[0] - body_rows
        tile = jnp.concatenate([cand_ref[k].astype(F32), jnp.zeros((tail - 2, 128), F32)], axis=0)
        outs[k][body_rows : body_rows + tail, :] = tile.astype(jnp.bfloat16)
    for copy in copies:
        copy.wait()


def frames_kernel(win_ref, out_ref, tab_ref):
    low = iota((P_SIZE, 128), 1) < 64

    def rows_of(seam, m):
        line = [
            win_ref[seam, :, pl.ds(pl.multiple_of(m * 384 + c * 128, 128), 128)].astype(F32)
            for c in range(3)
        ]
        last = pltpu.roll(line[2], 64, 1)
        middle = jnp.where(low, pltpu.roll(line[1], 64, 1), last)
        spot = seam * P_SIZE * PITCH + 2 * m
        for shift, value in ((0, line[0]), (1, middle), (WIN, line[1]), (WIN + 1, last)):
            for half in range(2):
                at = spot + half * 8 * PITCH + shift
                out_ref[pl.ds(at, 8, stride=PITCH), :] = value[8 * half : 8 * half + 8]
        return (line[0], line[1]), (middle, last)

    def grown(sums, row):
        left, right = row
        return (sums[0] + left, sums[1] + right, sums[2] + left * left, sums[3] + right * right)

    def put(seam, top, sums, add):
        for k in range(4):
            for half in range(2):
                at = (seam * P_SIZE + 8 * half) * TAB + k * TOPS + top
                spot = pl.ds(at, 8, stride=TAB)
                value = sums[k][8 * half : 8 * half + 8]
                tab_ref[spot, :] = tab_ref[spot, :] + value if add else value

    for seam in range(2):

        def always(i, sums, seam=seam):
            even, odd = rows_of(seam, 32 + i)
            return grown(grown(sums, even), odd)

        def above(i, sums, seam=seam):
            even, odd = rows_of(seam, 31 - i)
            sums = grown(sums, odd)
            put(seam, 63 - 2 * i, sums, False)
            sums = grown(sums, even)
            put(seam, 62 - 2 * i, sums, False)
            return sums

        def below(i, sums, seam=seam):
            even, odd = rows_of(seam, 64 + i)
            sums = grown(sums, even)
            put(seam, 2 * i + 1, sums, True)
            sums = grown(sums, odd)
            put(seam, 2 * i + 2, sums, True)
            return sums

        none = (jnp.zeros((P_SIZE, 128), F32),) * 4
        sums = lax.fori_loop(0, 32, always, none, unroll=16)
        put(seam, 64, sums, False)
        lax.fori_loop(0, 32, above, sums, unroll=16)
        lax.fori_loop(0, 32, below, none, unroll=16)


def springs_kernel(edges_ref, stiff_ref, live_ref, out_ref, ends_scr, stiff_scr):
    ends_scr[...] = jnp.zeros_like(ends_scr)
    stiff_scr[...] = jnp.zeros_like(stiff_scr)
    ends_scr[0:2, 0:E] = edges_ref[...]
    stiff_scr[0:1, 0:E] = stiff_ref[...]
    first, second = ends_scr[0:1], ends_scr[1:2]
    low, high = jnp.minimum(first, second), jnp.maximum(first, second)
    gap = high - low
    kind = jnp.where(gap == 1, 0, jnp.where(gap == GV, 1, jnp.where(gap == GV + 1, 2, 3)))
    left = jnp.where(iota((GV, E_PAD), 0) == (low >> 4), stiff_scr[0:1], 0.0)
    right = (iota((128, E_PAD), 0) == kind * GV + (low & (GV - 1))).astype(F32)
    out_ref[0:GV, :] = nt_dot(left, right)
    tile_row, tile_col = lax.axis_index("row"), lax.axis_index("col")
    for seam, (near_row, near_col) in enumerate(((tile_row, tile_col - 1), (tile_row - 1, tile_col))):
        counts = live_ref[jnp.maximum(near_row, 0), seam : seam + 1, :]
        wanted = (iota(counts.shape, 1) == near_col) & (near_row >= 0)
        count = jnp.sum(jnp.where(wanted, counts.astype(F32), 0.0), axis=1, keepdims=True)
        out_ref[GV + seam : GV + seam + 1, :] = jnp.broadcast_to(count, (1, 128))
    out_ref[GV + 2 : GV + 8, :] = jnp.zeros((6, 128), F32)


def split3(x):
    first = x.astype(jnp.bfloat16)
    rest = x - first.astype(F32)
    second = rest.astype(jnp.bfloat16)
    third = (rest - second.astype(F32)).astype(jnp.bfloat16)
    return first, second, third


def fold(x):
    pieces = [x[8 * t : 8 * t + 8] for t in range(x.shape[0] // 8)]
    while len(pieces) > 1:
        pieces = [a + b for a, b in zip(pieces[::2], pieces[1::2])]
    return pieces[0]


def match_kernel(seam, springs_ref, sent_ref, frame_ref, tab_ref, *rest):
    if seam == 0:
        other_ref, out_ref, a_scr, t_scr, s_scr, list_scr, cand_s, sem = rest
    else:
        out_ref, a_scr, t_scr, s_scr, list_scr, cand_s, sem = rest
    lists = sent_ref[P_SIZE * PATCH : P_SIZE * PATCH + 16, :].astype(F32)
    list_scr[...] = lists[0:8].astype(jnp.int32)
    copy = pltpu.make_async_copy(list_scr, cand_s, sem)
    copy.start()

    def one_sum(p, carry):
        pixels = sent_ref[pl.ds(pl.multiple_of(p * PATCH, PATCH), PATCH), :].astype(F32)
        spot = pl.multiple_of(p * 8, 8)
        for q, part in ((3, fold(pixels)), (4, fold(pixels * pixels))):
            s_scr[pl.ds(q * 128 + spot, 8), :] = jnp.broadcast_to(
                jnp.sum(part, axis=0, keepdims=True), (8, 128)
            )
        return carry

    lax.fori_loop(0, P_SIZE, one_sum, 0, unroll=2)
    copy.wait()
    count = springs_ref[GV + seam : GV + seam + 1, 0:1].astype(jnp.int32)
    lane = iota((8, 128), 1)
    full_lane = iota((PATCH, 128), 1)
    row = iota((8, 128), 0)

    def one_patch(p, carry):
        pixels = sent_ref[pl.ds(pl.multiple_of(p * PATCH, PATCH), PATCH), :]
        a_scr[...] = pixels.astype(F32)
        base = (seam * P_SIZE + p) * PITCH
        for s in range(NS):
            move_y = cand_s[0, p * NS + s] + REACH
            top = base + move_y
            move_x = cand_s[1, p * NS + s] + REACH
            crop = jnp.where(
                full_lane < move_x,
                frame_ref[pl.ds(top + WIN, PATCH), :],
                frame_ref[pl.ds(top, PATCH), :],
            )
            cross = fold(pltpu.roll(a_scr[...], move_x, 1) * crop)
            t_scr[9 * s : 9 * s + 8, :] = cross
            at = (seam * P_SIZE + p) * TAB + move_y
            for q in range(2):
                line = jnp.where(
                    full_lane[0:1] < move_x,
                    tab_ref[pl.ds(at + (2 * q + 1) * TOPS, 1), :],
                    tab_ref[pl.ds(at + 2 * q * TOPS, 1), :],
                )
                s_scr[pl.ds((q + 1) * 128 + p * 8 + s, 1), :] = line
        part = t_scr[pl.ds(0, 8, stride=9), :]
        for k in range(1, 8):
            part = part + t_scr[pl.ds(k, 8, stride=9), :]
        s_scr[pl.ds(pl.multiple_of(p * 8, 8), 8), :] = part
        return carry

    lax.fori_loop(0, P_SIZE, one_patch, 0, unroll=4)
    cross, total, square, a_sum, a_sq = (
        jnp.sum(s_scr[128 * q : 128 * q + 128, :].T, axis=0, keepdims=True) / PIXELS
        for q in range(5)
    )
    cov = cross - a_sum * total
    var_a = a_sq - a_sum * a_sum
    var_b = square - total * total
    ncc = cov / jnp.sqrt((var_a + EPSILON) * (var_b + EPSILON))
    weight = jnp.where((lane[0:1] >> 3) < count, (1.5 + ncc) * (1.5 + ncc), 0.0)
    parts = jnp.where(
        row == 0,
        weight,
        jnp.where(row == 1, weight * lists[0:1], jnp.where(row == 2, weight * lists[1:2], 0.0)),
    )
    group = ((iota((128, 128), 0) >> 3) == iota((128, 128), 1)).astype(jnp.bfloat16)
    sums = [jnp.dot(part, group, preferred_element_type=F32) for part in split3(parts)]
    sums = sums[0] + sums[1] + sums[2]

    def estimates(w_sum, w_y, w_x, slot):
        alive = slot < count
        conf = jnp.where(alive, w_sum / NS, 0.0)
        along_y = jnp.where(alive, w_y / (REACH * w_sum), 0.0)
        along_x = jnp.where(alive, w_x / (REACH * w_sum), 0.0)
        return conf, along_y, along_x

    conf, along_y, along_x = estimates(sums[0:1], sums[1:2], sums[2:3], lane[0:1])
    if seam == 1:
        lines = (conf, conf * along_y, conf * along_x, along_y, along_x)
        for k, line in enumerate(lines):
            out_ref[k : k + 1, :] = line
        out_ref[5:8, :] = jnp.zeros((3, 128), F32)
    else:
        lines = (conf, conf * along_y, conf * along_x)
        cols = jnp.concatenate(lines + (jnp.zeros((5, 128), F32),), axis=0).T
        lane16 = iota((16, 128), 1)
        block = springs_ref[0:GV, :]
        for k in range(3):
            block = jnp.where(lane16 == 64 + k, cols[0:16, k : k + 1], block)
        out_ref[0:16, :] = block
        out_ref[16:24, :] = other_ref[...]
        for k, line in enumerate((along_y, along_x, conf)):
            out_ref[21 + k : 22 + k, :] = line


def krylov_kernel(inner_ref, centre_ref, outer_ref, u_ref, mom_ref, match_ref):
    odd = lax.axis_index("col") % 2 == 1
    west = jnp.where(odd, inner_ref[...], outer_ref[...])
    east = jnp.where(odd, outer_ref[...], inner_ref[...])
    tiles = (west, centre_ref[...], east)
    lane = iota((48, 128), 1)
    row = iota((48, 128), 0)
    blocks = [jnp.concatenate([tile[a, 0:16, :] for a in range(3)], axis=0) for tile in tiles]

    def both(x):
        return x + pltpu.roll(x, 64, 1)

    def plane(t):
        out = jnp.zeros((48, 128), F32)
        for b in range(3):
            moved = pltpu.roll(blocks[b], (16 * b - 16 * t) % 128, 1)
            out = jnp.where((lane >> 4) == b, moved, out)
        return both(out)

    def west_seam(lane_y, lane_x):
        out = jnp.zeros((48, 128), F32)
        for b in (1, 2):
            out = jnp.where(lane == 16 * b - 1, blocks[b][:, lane_y : lane_y + 1], out)
            out = jnp.where(lane == 16 * b + 63, blocks[b][:, lane_x : lane_x + 1], out)
        return out

    def north_lines(a, r):
        lines = [tile[a, r : r + 1, :] for tile in tiles]
        return lines[0] + pltpu.roll(lines[1], 16, 1) + pltpu.roll(lines[2], 32, 1)

    def north_seam(r_y, r_x):
        out = jnp.zeros((48, 128), F32)
        for a in (1, 2):
            line = north_lines(a, r_y) + pltpu.roll(north_lines(a, r_x), 64, 1)
            out = jnp.where(row == 16 * a - 1, line, out)
        return out

    q_h = plane(0) + west_seam(64, 64)
    q_v = plane(1) + north_seam(16, 16)
    q_d = plane(2)
    q_a = plane(3)
    f_h = west_seam(65, 66)
    f_v = north_seam(17, 18)

    def right(x):
        return pltpu.roll(x, 1, 1)

    def left(x):
        return pltpu.roll(x, 127, 1)

    def down(x):
        return pltpu.roll(x, 1, 0)

    def up(x):
        return pltpu.roll(x, 47, 0)

    def operate(v):
        below = up(v)
        h = q_h * (v - left(v))
        s = q_v * (v - below)
        d = q_d * (v - left(below))
        a = q_a * (v - right(below))
        out = (LAMBDA_REG - THETA) * v + (h + s) + (d + a)
        return out - right(h + down(d)) - down(s + left(a))

    u0 = f_h + f_v - right(f_h) - down(f_v)
    u1 = operate(u0)
    u2 = operate(u1)
    u3 = operate(u2)
    own = slice(16, 32)
    lane16 = lane[own]
    inside = ((lane16 >= 16) & (lane16 < 32)) | ((lane16 >= 80) & (lane16 < 96))
    parts = [jnp.where(inside, x[own], 0.0) for x in (u0, u1, u2, u3)]
    lane1 = iota((1, 128), 1)
    moments = jnp.zeros((1, 128), F32)
    for k in range(6):
        product = parts[k // 2] * parts[k // 2 + k % 2]
        value = jnp.sum(jnp.sum(product, axis=0, keepdims=True), axis=1, keepdims=True)
        moments = jnp.where(lane1 == k, value, moments)
    for k in range(3):
        u_ref[k] = parts[k]
    mom_ref[...] = jnp.broadcast_to(moments[None], mom_ref.shape)
    for k, (east_row, south_row) in enumerate(((21, 19), (22, 20), (23, 16))):
        match_ref[k, 0:1, :] = east[1, east_row : east_row + 1, 0:16]
        match_ref[k, 1:2, :] = centre_ref[2, south_row : south_row + 1, 0:16]


def flatten_kernel(u_ref, out_ref):
    vertex = iota((128, 256), 1)
    source = iota((128, 256), 0)
    fields = jnp.concatenate([u_ref[k] for k in range(3)], axis=0)
    keep = iota((16, 256), 0) == (iota((16, 256), 1) >> 4)
    for comp in range(2):
        spread = (source == (vertex & 15) + (16 + 64 * comp)).astype(F32)
        wide = jnp.dot(fields, spread, precision=PRECISE, preferred_element_type=F32)
        for k in range(3):
            line = jnp.where(keep, wide[16 * k : 16 * k + 16], 0.0)
            out_ref[k, comp : comp + 1, :] = jnp.sum(line, axis=0, keepdims=True)


def combine_kernel(mom_ref, u_ref, out_ref):
    total = jnp.sum(mom_ref[...], axis=0, keepdims=True)
    lane = iota((1, 128), 1)
    m = [
        jnp.broadcast_to(
            jnp.sum(jnp.where(lane == k, total, 0.0), axis=1, keepdims=True), (1, 128)
        )
        for k in range(6)
    ]

    def gram(p, lift):
        out = None
        for i in range(3):
            for j in range(i, 3):
                if p[i] is None or p[j] is None:
                    continue
                term = m[i + j]
                if lift:
                    term = m[i + j + 1] + THETA * term
                term = (term * p[i]) * p[j]
                if j > i:
                    term = term + term
                out = term if out is None else out + term
        return out

    one = jnp.ones((1, 128), F32)
    r = [one, None, None]
    d = r
    rr = m[0]
    x = [None, None, None]

    def plus(a, b):
        return b if a is None else a if b is None else a + b

    def times(s, a):
        return None if a is None else s * a

    for step in range(3):
        alpha = rr / gram(d, True)
        x = [plus(x[i], times(alpha, d[i])) for i in range(3)]
        if step == 2:
            break
        image = [times(THETA, d[0]), plus(d[0], times(THETA, d[1])), plus(d[1], times(THETA, d[2]))]
        r = [plus(r[i], times(-alpha, image[i])) for i in range(3)]
        new = gram(r, False)
        d = [plus(r[i], times(new / rr, d[i])) for i in range(3)]
        rr = new
    wide = [jnp.concatenate([c, c], axis=1) for c in x]
    out_ref[...] = wide[0] * u_ref[0] + wide[1] * u_ref[1] + wide[2] * u_ref[2]


def limit(mib):
    return pltpu.CompilerParams(vmem_limit_bytes=mib * 1024 * 1024)


def shape(dims, dtype=F32):
    return jax.ShapeDtypeStruct(dims, dtype)


def swaps(x, axis):
    length = lax.axis_size(axis)
    inner = [(i, i ^ 1) for i in range(length)]
    outer = [(i, i + 1 if i % 2 else i - 1) for i in range(1, length - 1)]
    return lax.ppermute(x, axis, inner), lax.ppermute(x, axis, outer)


def call_pack(patches, candidates):
    return pl.pallas_call(
        pack_kernel,
        out_shape=tuple(
            shape((P_SIZE * PATCH + tail, 128), jnp.bfloat16) for tail in (32, 16)
        ),
        in_specs=[HBM, VMEM],
        out_specs=(VMEM, VMEM),
        scratch_shapes=[pltpu.SemaphoreType.DMA((2,))],
        compiler_params=limit(4),
    )(patches, candidates)


def call_frames(windows):
    return pl.pallas_call(
        frames_kernel,
        out_shape=(shape((2 * P_SIZE * PITCH, 128)), shape((2 * P_SIZE * TAB, 128))),
        in_specs=[VMEM],
        out_specs=(VMEM, VMEM),
        compiler_params=limit(16),
    )(windows)


def call_match(seam, *operands):
    return pl.pallas_call(
        functools.partial(match_kernel, seam),
        out_shape=shape((24 if seam == 0 else 8, 128)),
        in_specs=[VMEM] * len(operands),
        out_specs=VMEM,
        scratch_shapes=[
            pltpu.VMEM((128, 128), F32),
            pltpu.VMEM((72, 128), F32),
            pltpu.VMEM((640, 128), F32),
            pltpu.VMEM((8, 128), jnp.int32),
            pltpu.SMEM((8, 128), jnp.int32),
            pltpu.SemaphoreType.DMA,
        ],
        compiler_params=limit(14),
    )(*operands)


def body(patches, windows, candidates, live, edges, stiffness):
    to_east, to_south = call_pack(patches.reshape(2, P_SIZE * PATCH, PATCH), candidates[0, 0])
    sent_west = shifted(to_east, "col", 1)
    sent_north = shifted(to_south, "row", 1)

    frames, table = call_frames(windows[0, 0])
    springs = pl.pallas_call(
        springs_kernel,
        out_shape=shape((GV + 8, 128)),
        in_specs=[VMEM, VMEM, VMEM],
        out_specs=VMEM,
        scratch_shapes=[pltpu.VMEM((8, E_PAD), jnp.int32), pltpu.VMEM((8, E_PAD), F32)],
        compiler_params=limit(4),
    )(edges[0], stiffness, live.transpose(0, 2, 1))
    seam_north = call_match(1, springs, sent_north, frames, table)
    own = call_match(0, springs, sent_west, frames, table, seam_north)
    inner, outer = swaps(own, "row")
    odd = lax.axis_index("row") % 2 == 1
    centre = jnp.stack([jnp.where(odd, inner, outer), own, jnp.where(odd, outer, inner)])
    inner, outer = swaps(centre, "col")
    devices = lax.axis_size("row") * lax.axis_size("col")
    basis, moments, matches = pl.pallas_call(
        krylov_kernel,
        out_shape=(shape((3, 16, 128)), shape((devices, 1, 128)), shape((3, 2, P_SIZE))),
        in_specs=[VMEM] * 3,
        out_specs=(VMEM, VMEM, VMEM),
        compiler_params=limit(4),
    )(inner, centre, outer)
    moments = lax.all_to_all(moments, ("row", "col"), 0, 0).reshape(devices, 128)
    flat = pl.pallas_call(
        flatten_kernel,
        out_shape=shape((3, 2, GV * GV)),
        in_specs=[VMEM],
        out_specs=VMEM,
        compiler_params=limit(4),
    )(basis)
    mesh_shift = pl.pallas_call(
        combine_kernel,
        out_shape=shape((2, GV * GV)),
        in_specs=[VMEM, VMEM],
        out_specs=VMEM,
        compiler_params=limit(4),
    )(moments, flat)
    return matches.transpose(1, 0, 2)[None, None], mesh_shift[None, None]


def solution(mesh):
    return jax.shard_map(
        body,
        mesh=mesh,
        in_specs=(
            P("row", "col", None, None, None, None),
            P("row", "col", None, None, None),
            P("row", "col", None, None, None),
            P(),
            P("row", None, "col"),
            P("row", "col"),
        ),
        out_specs=(P("row", "col", None, None, None), P("row", "col", None, None)),
        check_vma=False,
    )
```

```python
import functools

import jax
import jax.numpy as jnp
from jax import lax
from jax.experimental import pallas as pl
from jax.experimental.pallas import tpu as pltpu
from jax.sharding import PartitionSpec as P

PATCH = 128
REACH = 32
WIN = 192
NS = 8
P_SIZE = 16
GV = 16
E = 705
E_PAD = 768
PITCH = 2 * WIN + 1
TOPS = WIN - PATCH + 1
TAB = 4 * TOPS + 1
PIXELS = float(PATCH * PATCH)
LAMBDA_REG = 0.05
EPSILON = 1e-05
THETA = 8.0
PRECISE = lax.Precision.HIGHEST
F32 = jnp.float32
VMEM = pl.BlockSpec(memory_space=pltpu.VMEM)
HBM = pl.BlockSpec(memory_space=pltpu.HBM)


def shifted(x, axis, by):
    length = lax.axis_size(axis)
    pairs = [(i, i + by) for i in range(length) if 0 <= i + by < length]
    return lax.ppermute(x, axis, pairs)


def iota(shape, dim):
    return lax.broadcasted_iota(jnp.int32, shape, dim)


def nt_dot(a, b):
    return lax.dot_general(
        a, b, (((1,), (1,)), ((), ())), precision=PRECISE, preferred_element_type=F32
    )


def pack_kernel(patch_ref, cand_ref, east_ref, south_ref, sems):
    outs = (east_ref, south_ref)
    body_rows = P_SIZE * PATCH
    copies = [
        pltpu.make_async_copy(patch_ref.at[k], outs[k].at[pl.ds(0, body_rows)], sems.at[k])
        for k in range(2)
    ]
    for copy in copies:
        copy.start()
    for k in range(2):
        tail = outs[k].shape[0] - body_rows
        tile = jnp.concatenate([cand_ref[k].astype(F32), jnp.zeros((tail - 2, 128), F32)], axis=0)
        outs[k][body_rows : body_rows + tail, :] = tile.astype(jnp.bfloat16)
    for copy in copies:
        copy.wait()


def frames_kernel(win_ref, out_ref, tab_ref):
    low = iota((P_SIZE, 128), 1) < 64

    def rows_of(seam, m):
        line = [
            win_ref[seam, :, pl.ds(pl.multiple_of(m * 384 + c * 128, 128), 128)].astype(F32)
            for c in range(3)
        ]
        last = pltpu.roll(line[2], 64, 1)
        middle = jnp.where(low, pltpu.roll(line[1], 64, 1), last)
        spot = seam * P_SIZE * PITCH + 2 * m
        for shift, value in ((0, line[0]), (1, middle), (WIN, line[1]), (WIN + 1, last)):
            for half in range(2):
                at = spot + half * 8 * PITCH + shift
                out_ref[pl.ds(at, 8, stride=PITCH), :] = value[8 * half : 8 * half + 8]
        return (line[0], line[1]), (middle, last)

    def grown(sums, row):
        left, right = row
        return (sums[0] + left, sums[1] + right, sums[2] + left * left, sums[3] + right * right)

    def put(seam, top, sums, add):
        for k in range(4):
            for half in range(2):
                at = (seam * P_SIZE + 8 * half) * TAB + k * TOPS + top
                spot = pl.ds(at, 8, stride=TAB)
                value = sums[k][8 * half : 8 * half + 8]
                tab_ref[spot, :] = tab_ref[spot, :] + value if add else value

    for seam in range(2):

        def always(i, sums, seam=seam):
            even, odd = rows_of(seam, 32 + i)
            return grown(grown(sums, even), odd)

        def above(i, sums, seam=seam):
            even, odd = rows_of(seam, 31 - i)
            sums = grown(sums, odd)
            put(seam, 63 - 2 * i, sums, False)
            sums = grown(sums, even)
            put(seam, 62 - 2 * i, sums, False)
            return sums

        def below(i, sums, seam=seam):
            even, odd = rows_of(seam, 64 + i)
            sums = grown(sums, even)
            put(seam, 2 * i + 1, sums, True)
            sums = grown(sums, odd)
            put(seam, 2 * i + 2, sums, True)
            return sums

        none = (jnp.zeros((P_SIZE, 128), F32),) * 4
        sums = lax.fori_loop(0, 32, always, none, unroll=16)
        put(seam, 64, sums, False)
        lax.fori_loop(0, 32, above, sums, unroll=16)
        lax.fori_loop(0, 32, below, none, unroll=16)


def springs_kernel(edges_ref, stiff_ref, live_ref, out_ref, ends_scr, stiff_scr):
    ends_scr[...] = jnp.zeros_like(ends_scr)
    stiff_scr[...] = jnp.zeros_like(stiff_scr)
    ends_scr[0:2, 0:E] = edges_ref[...]
    stiff_scr[0:1, 0:E] = stiff_ref[...]
    first, second = ends_scr[0:1], ends_scr[1:2]
    low, high = jnp.minimum(first, second), jnp.maximum(first, second)
    gap = high - low
    kind = jnp.where(gap == 1, 0, jnp.where(gap == GV, 1, jnp.where(gap == GV + 1, 2, 3)))
    left = jnp.where(iota((GV, E_PAD), 0) == (low >> 4), stiff_scr[0:1], 0.0)
    right = (iota((128, E_PAD), 0) == kind * GV + (low & (GV - 1))).astype(F32)
    out_ref[0:GV, :] = nt_dot(left, right)
    tile_row, tile_col = lax.axis_index("row"), lax.axis_index("col")
    for seam, (near_row, near_col) in enumerate(((tile_row, tile_col - 1), (tile_row - 1, tile_col))):
        counts = live_ref[jnp.maximum(near_row, 0), seam : seam + 1, :]
        wanted = (iota(counts.shape, 1) == near_col) & (near_row >= 0)
        count = jnp.sum(jnp.where(wanted, counts.astype(F32), 0.0), axis=1, keepdims=True)
        out_ref[GV + seam : GV + seam + 1, :] = jnp.broadcast_to(count, (1, 128))
    out_ref[GV + 2 : GV + 8, :] = jnp.zeros((6, 128), F32)


def split3(x):
    first = x.astype(jnp.bfloat16)
    rest = x - first.astype(F32)
    second = rest.astype(jnp.bfloat16)
    third = (rest - second.astype(F32)).astype(jnp.bfloat16)
    return first, second, third


def fold(x):
    pieces = [x[8 * t : 8 * t + 8] for t in range(x.shape[0] // 8)]
    while len(pieces) > 1:
        pieces = [a + b for a, b in zip(pieces[::2], pieces[1::2])]
    return pieces[0]


def match_kernel(seam, springs_ref, sent_ref, frame_ref, tab_ref, *rest):
    if seam == 0:
        other_ref, out_ref, a_scr, t_scr, s_scr, list_scr, cand_s, sem = rest
    else:
        out_ref, a_scr, t_scr, s_scr, list_scr, cand_s, sem = rest
    lists = sent_ref[P_SIZE * PATCH : P_SIZE * PATCH + 16, :].astype(F32)
    list_scr[...] = lists[0:8].astype(jnp.int32)
    copy = pltpu.make_async_copy(list_scr, cand_s, sem)
    copy.start()

    def one_sum(p, carry):
        pixels = sent_ref[pl.ds(pl.multiple_of(p * PATCH, PATCH), PATCH), :].astype(F32)
        spot = pl.multiple_of(p * 8, 8)
        for q, part in ((3, fold(pixels)), (4, fold(pixels * pixels))):
            s_scr[pl.ds(q * 128 + spot, 8), :] = jnp.broadcast_to(
                jnp.sum(part, axis=0, keepdims=True), (8, 128)
            )
        return carry

    lax.fori_loop(0, P_SIZE, one_sum, 0, unroll=2)
    copy.wait()
    count = springs_ref[GV + seam : GV + seam + 1, 0:1].astype(jnp.int32)
    lane = iota((8, 128), 1)
    full_lane = iota((PATCH, 128), 1)
    row = iota((8, 128), 0)

    def one_patch(p, carry):
        pixels = sent_ref[pl.ds(pl.multiple_of(p * PATCH, PATCH), PATCH), :]
        a_scr[...] = pixels.astype(F32)
        base = (seam * P_SIZE + p) * PITCH
        for s in range(NS):
            move_y = cand_s[0, p * NS + s] + REACH
            top = base + move_y
            move_x = cand_s[1, p * NS + s] + REACH
            crop = jnp.where(
                full_lane < move_x,
                frame_ref[pl.ds(top + WIN, PATCH), :],
                frame_ref[pl.ds(top, PATCH), :],
            )
            cross = fold(pltpu.roll(a_scr[...], move_x, 1) * crop)
            t_scr[9 * s : 9 * s + 8, :] = cross
            at = (seam * P_SIZE + p) * TAB + move_y
            for q in range(2):
                line = jnp.where(
                    full_lane[0:1] < move_x,
                    tab_ref[pl.ds(at + (2 * q + 1) * TOPS, 1), :],
                    tab_ref[pl.ds(at + 2 * q * TOPS, 1), :],
                )
                s_scr[pl.ds((q + 1) * 128 + p * 8 + s, 1), :] = line
        part = t_scr[pl.ds(0, 8, stride=9), :]
        for k in range(1, 8):
            part = part + t_scr[pl.ds(k, 8, stride=9), :]
        s_scr[pl.ds(pl.multiple_of(p * 8, 8), 8), :] = part
        return carry

    lax.fori_loop(0, P_SIZE, one_patch, 0, unroll=8)
    cross, total, square, a_sum, a_sq = (
        jnp.sum(s_scr[128 * q : 128 * q + 128, :].T, axis=0, keepdims=True) / PIXELS
        for q in range(5)
    )
    cov = cross - a_sum * total
    var_a = a_sq - a_sum * a_sum
    var_b = square - total * total
    ncc = cov / jnp.sqrt((var_a + EPSILON) * (var_b + EPSILON))
    weight = jnp.where((lane[0:1] >> 3) < count, (1.5 + ncc) * (1.5 + ncc), 0.0)
    parts = jnp.where(
        row == 0,
        weight,
        jnp.where(row == 1, weight * lists[0:1], jnp.where(row == 2, weight * lists[1:2], 0.0)),
    )
    group = ((iota((128, 128), 0) >> 3) == iota((128, 128), 1)).astype(jnp.bfloat16)
    sums = [jnp.dot(part, group, preferred_element_type=F32) for part in split3(parts)]
    sums = sums[0] + sums[1] + sums[2]

    def estimates(w_sum, w_y, w_x, slot):
        alive = slot < count
        conf = jnp.where(alive, w_sum / NS, 0.0)
        along_y = jnp.where(alive, w_y / (REACH * w_sum), 0.0)
        along_x = jnp.where(alive, w_x / (REACH * w_sum), 0.0)
        return conf, along_y, along_x

    conf, along_y, along_x = estimates(sums[0:1], sums[1:2], sums[2:3], lane[0:1])
    if seam == 1:
        lines = (conf, conf * along_y, conf * along_x, along_y, along_x)
        for k, line in enumerate(lines):
            out_ref[k : k + 1, :] = line
        out_ref[5:8, :] = jnp.zeros((3, 128), F32)
    else:
        lines = (conf, conf * along_y, conf * along_x)
        cols = jnp.concatenate(lines + (jnp.zeros((5, 128), F32),), axis=0).T
        lane16 = iota((16, 128), 1)
        block = springs_ref[0:GV, :]
        for k in range(3):
            block = jnp.where(lane16 == 64 + k, cols[0:16, k : k + 1], block)
        out_ref[0:16, :] = block
        out_ref[16:24, :] = other_ref[...]
        for k, line in enumerate((along_y, along_x, conf)):
            out_ref[21 + k : 22 + k, :] = line


def krylov_kernel(inner_ref, centre_ref, outer_ref, u_ref, mom_ref, match_ref):
    odd = lax.axis_index("col") % 2 == 1
    west = jnp.where(odd, inner_ref[...], outer_ref[...])
    east = jnp.where(odd, outer_ref[...], inner_ref[...])
    tiles = (west, centre_ref[...], east)
    lane = iota((32, 128), 1)
    row = iota((32, 128), 0)
    spans = (slice(8, 16), slice(0, 16), slice(0, 8))
    blocks = [
        jnp.concatenate([tile[a, spans[a], :] for a in range(3)], axis=0) for tile in tiles
    ]

    def both(x):
        return x + pltpu.roll(x, 64, 1)

    def plane(t):
        out = jnp.zeros((32, 128), F32)
        for b in range(3):
            moved = pltpu.roll(blocks[b], (16 * b - 16 * t) % 128, 1)
            out = jnp.where((lane >> 4) == b, moved, out)
        return both(out)

    def west_seam(lane_y, lane_x):
        out = jnp.zeros((32, 128), F32)
        for b in (1, 2):
            out = jnp.where(lane == 16 * b - 1, blocks[b][:, lane_y : lane_y + 1], out)
            out = jnp.where(lane == 16 * b + 63, blocks[b][:, lane_x : lane_x + 1], out)
        return out

    def north_lines(a, r):
        lines = [tile[a, r : r + 1, :] for tile in tiles]
        return lines[0] + pltpu.roll(lines[1], 16, 1) + pltpu.roll(lines[2], 32, 1)

    def north_seam(r_y, r_x):
        out = jnp.zeros((32, 128), F32)
        for a in (1, 2):
            line = north_lines(a, r_y) + pltpu.roll(north_lines(a, r_x), 64, 1)
            out = jnp.where(row == 16 * a - 9, line, out)
        return out

    q_h = plane(0) + west_seam(64, 64)
    q_v = plane(1) + north_seam(16, 16)
    q_d = plane(2)
    q_a = plane(3)
    f_h = west_seam(65, 66)
    f_v = north_seam(17, 18)

    def right(x):
        return pltpu.roll(x, 1, 1)

    def left(x):
        return pltpu.roll(x, 127, 1)

    def down(x):
        return pltpu.roll(x, 1, 0)

    def up(x):
        return pltpu.roll(x, 31, 0)

    def operate(v):
        below = up(v)
        h = q_h * (v - left(v))
        s = q_v * (v - below)
        d = q_d * (v - left(below))
        a = q_a * (v - right(below))
        out = (LAMBDA_REG - THETA) * v + (h + s) + (d + a)
        return out - right(h + down(d)) - down(s + left(a))

    u0 = f_h + f_v - right(f_h) - down(f_v)
    u1 = operate(u0)
    u2 = operate(u1)
    u3 = operate(u2)
    own = slice(8, 24)
    lane16 = lane[own]
    inside = ((lane16 >= 16) & (lane16 < 32)) | ((lane16 >= 80) & (lane16 < 96))
    parts = [jnp.where(inside, x[own], 0.0) for x in (u0, u1, u2, u3)]
    lane1 = iota((1, 128), 1)
    moments = jnp.zeros((1, 128), F32)
    for k in range(6):
        product = parts[k // 2] * parts[k // 2 + k % 2]
        value = jnp.sum(jnp.sum(product, axis=0, keepdims=True), axis=1, keepdims=True)
        moments = jnp.where(lane1 == k, value, moments)
    for k in range(3):
        u_ref[k] = parts[k]
    mom_ref[...] = jnp.broadcast_to(moments[None], mom_ref.shape)
    for k, (east_row, south_row) in enumerate(((21, 19), (22, 20), (23, 16))):
        match_ref[k, 0:1, :] = east[1, east_row : east_row + 1, 0:16]
        match_ref[k, 1:2, :] = centre_ref[2, south_row : south_row + 1, 0:16]


def flatten_kernel(u_ref, out_ref):
    vertex = iota((128, 256), 1)
    source = iota((128, 256), 0)
    fields = jnp.concatenate([u_ref[k] for k in range(3)], axis=0)
    keep = iota((16, 256), 0) == (iota((16, 256), 1) >> 4)
    for comp in range(2):
        spread = (source == (vertex & 15) + (16 + 64 * comp)).astype(F32)
        wide = jnp.dot(fields, spread, precision=PRECISE, preferred_element_type=F32)
        for k in range(3):
            line = jnp.where(keep, wide[16 * k : 16 * k + 16], 0.0)
            out_ref[k, comp : comp + 1, :] = jnp.sum(line, axis=0, keepdims=True)


def combine_kernel(mom_ref, u_ref, out_ref):
    total = jnp.sum(mom_ref[...], axis=0, keepdims=True)
    lane = iota((1, 128), 1)
    m = [
        jnp.broadcast_to(
            jnp.sum(jnp.where(lane == k, total, 0.0), axis=1, keepdims=True), (1, 128)
        )
        for k in range(6)
    ]

    def gram(p, lift):
        out = None
        for i in range(3):
            for j in range(i, 3):
                if p[i] is None or p[j] is None:
                    continue
                term = m[i + j]
                if lift:
                    term = m[i + j + 1] + THETA * term
                term = (term * p[i]) * p[j]
                if j > i:
                    term = term + term
                out = term if out is None else out + term
        return out

    one = jnp.ones((1, 128), F32)
    r = [one, None, None]
    d = r
    rr = m[0]
    x = [None, None, None]

    def plus(a, b):
        return b if a is None else a if b is None else a + b

    def times(s, a):
        return None if a is None else s * a

    for step in range(3):
        alpha = rr / gram(d, True)
        x = [plus(x[i], times(alpha, d[i])) for i in range(3)]
        if step == 2:
            break
        image = [times(THETA, d[0]), plus(d[0], times(THETA, d[1])), plus(d[1], times(THETA, d[2]))]
        r = [plus(r[i], times(-alpha, image[i])) for i in range(3)]
        new = gram(r, False)
        d = [plus(r[i], times(new / rr, d[i])) for i in range(3)]
        rr = new
    wide = [jnp.concatenate([c, c], axis=1) for c in x]
    out_ref[...] = wide[0] * u_ref[0] + wide[1] * u_ref[1] + wide[2] * u_ref[2]


def limit(mib):
    return pltpu.CompilerParams(vmem_limit_bytes=mib * 1024 * 1024)


def shape(dims, dtype=F32):
    return jax.ShapeDtypeStruct(dims, dtype)


def swaps(x, axis):
    length = lax.axis_size(axis)
    inner = [(i, i ^ 1) for i in range(length)]
    outer = [(i, i + 1 if i % 2 else i - 1) for i in range(1, length - 1)]
    return lax.ppermute(x, axis, inner), lax.ppermute(x, axis, outer)


def call_pack(patches, candidates):
    return pl.pallas_call(
        pack_kernel,
        out_shape=tuple(
            shape((P_SIZE * PATCH + tail, 128), jnp.bfloat16) for tail in (32, 16)
        ),
        in_specs=[HBM, VMEM],
        out_specs=(VMEM, VMEM),
        scratch_shapes=[pltpu.SemaphoreType.DMA((2,))],
        compiler_params=limit(4),
    )(patches, candidates)


def call_frames(windows):
    return pl.pallas_call(
        frames_kernel,
        out_shape=(shape((2 * P_SIZE * PITCH, 128)), shape((2 * P_SIZE * TAB, 128))),
        in_specs=[VMEM],
        out_specs=(VMEM, VMEM),
        compiler_params=limit(16),
    )(windows)


def call_match(seam, *operands):
    return pl.pallas_call(
        functools.partial(match_kernel, seam),
        out_shape=shape((24 if seam == 0 else 8, 128)),
        in_specs=[VMEM] * len(operands),
        out_specs=VMEM,
        scratch_shapes=[
            pltpu.VMEM((128, 128), F32),
            pltpu.VMEM((72, 128), F32),
            pltpu.VMEM((640, 128), F32),
            pltpu.VMEM((8, 128), jnp.int32),
            pltpu.SMEM((8, 128), jnp.int32),
            pltpu.SemaphoreType.DMA,
        ],
        compiler_params=limit(14),
    )(*operands)


def body(patches, windows, candidates, live, edges, stiffness):
    to_east, to_south = call_pack(patches.reshape(2, P_SIZE * PATCH, PATCH), candidates[0, 0])
    sent_west = shifted(to_east, "col", 1)
    sent_north = shifted(to_south, "row", 1)

    frames, table = call_frames(windows[0, 0])
    springs = pl.pallas_call(
        springs_kernel,
        out_shape=shape((GV + 8, 128)),
        in_specs=[VMEM, VMEM, VMEM],
        out_specs=VMEM,
        scratch_shapes=[pltpu.VMEM((8, E_PAD), jnp.int32), pltpu.VMEM((8, E_PAD), F32)],
        compiler_params=limit(4),
    )(edges[0], stiffness, live.transpose(0, 2, 1))
    seam_north = call_match(1, springs, sent_north, frames, table)
    own = call_match(0, springs, sent_west, frames, table, seam_north)
    inner, outer = swaps(own, "row")
    odd = lax.axis_index("row") % 2 == 1
    centre = jnp.stack([jnp.where(odd, inner, outer), own, jnp.where(odd, outer, inner)])
    inner, outer = swaps(centre, "col")
    devices = lax.axis_size("row") * lax.axis_size("col")
    basis, moments, matches = pl.pallas_call(
        krylov_kernel,
        out_shape=(shape((3, 16, 128)), shape((devices, 1, 128)), shape((3, 2, P_SIZE))),
        in_specs=[VMEM] * 3,
        out_specs=(VMEM, VMEM, VMEM),
        compiler_params=limit(4),
    )(inner, centre, outer)
    moments = lax.all_to_all(moments, ("row", "col"), 0, 0).reshape(devices, 128)
    flat = pl.pallas_call(
        flatten_kernel,
        out_shape=shape((3, 2, GV * GV)),
        in_specs=[VMEM],
        out_specs=VMEM,
        compiler_params=limit(4),
    )(basis)
    mesh_shift = pl.pallas_call(
        combine_kernel,
        out_shape=shape((2, GV * GV)),
        in_specs=[VMEM, VMEM],
        out_specs=VMEM,
        compiler_params=limit(4),
    )(moments, flat)
    return matches.transpose(1, 0, 2)[None, None], mesh_shift[None, None]


def solution(mesh):
    return jax.shard_map(
        body,
        mesh=mesh,
        in_specs=(
            P("row", "col", None, None, None, None),
            P("row", "col", None, None, None),
            P("row", "col", None, None, None),
            P(),
            P("row", None, "col"),
            P("row", "col"),
        ),
        out_specs=(P("row", "col", None, None, None), P("row", "col", None, None)),
        check_vma=False,
    )
```

```python
import functools

import jax
import jax.numpy as jnp
from jax import lax
from jax.experimental import pallas as pl
from jax.experimental.pallas import tpu as pltpu
from jax.sharding import PartitionSpec as P

PATCH = 128
REACH = 32
WIN = 192
NS = 8
P_SIZE = 16
GV = 16
E = 705
E_PAD = 768
PITCH = 2 * WIN + 1
TOPS = WIN - PATCH + 1
TAB = 4 * TOPS + 1
PIXELS = float(PATCH * PATCH)
LAMBDA_REG = 0.05
EPSILON = 1e-05
THETA = 8.0
PRECISE = lax.Precision.HIGHEST
F32 = jnp.float32
VMEM = pl.BlockSpec(memory_space=pltpu.VMEM)
HBM = pl.BlockSpec(memory_space=pltpu.HBM)


def shifted(x, axis, by):
    length = lax.axis_size(axis)
    pairs = [(i, i + by) for i in range(length) if 0 <= i + by < length]
    return lax.ppermute(x, axis, pairs)


def iota(shape, dim):
    return lax.broadcasted_iota(jnp.int32, shape, dim)


def nt_dot(a, b):
    return lax.dot_general(
        a, b, (((1,), (1,)), ((), ())), precision=PRECISE, preferred_element_type=F32
    )


def pack_kernel(patch_ref, cand_ref, east_ref, south_ref, sems):
    outs = (east_ref, south_ref)
    body_rows = P_SIZE * PATCH
    copies = [
        pltpu.make_async_copy(patch_ref.at[k], outs[k].at[pl.ds(0, body_rows)], sems.at[k])
        for k in range(2)
    ]
    for copy in copies:
        copy.start()
    for k in range(2):
        tail = outs[k].shape[0] - body_rows
        tile = jnp.concatenate([cand_ref[k].astype(F32), jnp.zeros((tail - 2, 128), F32)], axis=0)
        outs[k][body_rows : body_rows + tail, :] = tile.astype(jnp.bfloat16)
    for copy in copies:
        copy.wait()


def frames_kernel(win_ref, out_ref, tab_ref):
    low = iota((P_SIZE, 128), 1) < 64

    def rows_of(seam, m):
        line = [
            win_ref[seam, :, pl.ds(pl.multiple_of(m * 384 + c * 128, 128), 128)].astype(F32)
            for c in range(3)
        ]
        last = pltpu.roll(line[2], 64, 1)
        middle = jnp.where(low, pltpu.roll(line[1], 64, 1), last)
        spot = seam * P_SIZE * PITCH + 2 * m
        for shift, value in ((0, line[0]), (1, middle), (WIN, line[1]), (WIN + 1, last)):
            for half in range(2):
                at = spot + half * 8 * PITCH + shift
                out_ref[pl.ds(at, 8, stride=PITCH), :] = value[8 * half : 8 * half + 8]
        return (line[0], line[1]), (middle, last)

    def grown(sums, row):
        left, right = row
        return (sums[0] + left, sums[1] + right, sums[2] + left * left, sums[3] + right * right)

    def put(seam, top, sums, add):
        for k in range(4):
            for half in range(2):
                at = (seam * P_SIZE + 8 * half) * TAB + k * TOPS + top
                spot = pl.ds(at, 8, stride=TAB)
                value = sums[k][8 * half : 8 * half + 8]
                tab_ref[spot, :] = tab_ref[spot, :] + value if add else value

    for seam in range(2):

        def always(i, sums, seam=seam):
            even, odd = rows_of(seam, 32 + i)
            return grown(grown(sums, even), odd)

        def above(i, sums, seam=seam):
            even, odd = rows_of(seam, 31 - i)
            sums = grown(sums, odd)
            put(seam, 63 - 2 * i, sums, False)
            sums = grown(sums, even)
            put(seam, 62 - 2 * i, sums, False)
            return sums

        def below(i, sums, seam=seam):
            even, odd = rows_of(seam, 64 + i)
            sums = grown(sums, even)
            put(seam, 2 * i + 1, sums, True)
            sums = grown(sums, odd)
            put(seam, 2 * i + 2, sums, True)
            return sums

        none = (jnp.zeros((P_SIZE, 128), F32),) * 4
        sums = lax.fori_loop(0, 32, always, none, unroll=16)
        put(seam, 64, sums, False)
        lax.fori_loop(0, 32, above, sums, unroll=16)
        lax.fori_loop(0, 32, below, none, unroll=16)


def springs_kernel(edges_ref, stiff_ref, live_ref, out_ref, ends_scr, stiff_scr):
    ends_scr[...] = jnp.zeros_like(ends_scr)
    stiff_scr[...] = jnp.zeros_like(stiff_scr)
    ends_scr[0:2, 0:E] = edges_ref[...]
    stiff_scr[0:1, 0:E] = stiff_ref[...]
    first, second = ends_scr[0:1], ends_scr[1:2]
    low, high = jnp.minimum(first, second), jnp.maximum(first, second)
    gap = high - low
    kind = jnp.where(gap == 1, 0, jnp.where(gap == GV, 1, jnp.where(gap == GV + 1, 2, 3)))
    left = jnp.where(iota((GV, E_PAD), 0) == (low >> 4), stiff_scr[0:1], 0.0)
    right = (iota((128, E_PAD), 0) == kind * GV + (low & (GV - 1))).astype(F32)
    out_ref[0:GV, :] = nt_dot(left, right)
    tile_row, tile_col = lax.axis_index("row"), lax.axis_index("col")
    for seam, (near_row, near_col) in enumerate(((tile_row, tile_col - 1), (tile_row - 1, tile_col))):
        counts = live_ref[jnp.maximum(near_row, 0), seam : seam + 1, :]
        wanted = (iota(counts.shape, 1) == near_col) & (near_row >= 0)
        count = jnp.sum(jnp.where(wanted, counts.astype(F32), 0.0), axis=1, keepdims=True)
        out_ref[GV + seam : GV + seam + 1, :] = jnp.broadcast_to(count, (1, 128))
    out_ref[GV + 2 : GV + 8, :] = jnp.zeros((6, 128), F32)


def split3(x):
    first = x.astype(jnp.bfloat16)
    rest = x - first.astype(F32)
    second = rest.astype(jnp.bfloat16)
    third = (rest - second.astype(F32)).astype(jnp.bfloat16)
    return first, second, third


def fold(x):
    pieces = [x[8 * t : 8 * t + 8] for t in range(x.shape[0] // 8)]
    while len(pieces) > 1:
        pieces = [a + b for a, b in zip(pieces[::2], pieces[1::2])]
    return pieces[0]


def match_kernel(seam, springs_ref, sent_ref, frame_ref, tab_ref, *rest):
    if seam == 0:
        other_ref, out_ref, a_scr, t_scr, s_scr, list_scr, cand_s, sem = rest
    else:
        out_ref, a_scr, t_scr, s_scr, list_scr, cand_s, sem = rest
    lists = sent_ref[P_SIZE * PATCH : P_SIZE * PATCH + 16, :].astype(F32)
    list_scr[...] = lists[0:8].astype(jnp.int32)
    copy = pltpu.make_async_copy(list_scr, cand_s, sem)
    copy.start()

    def one_sum(p, carry):
        pixels = sent_ref[pl.ds(pl.multiple_of(p * PATCH, PATCH), PATCH), :].astype(F32)
        spot = pl.multiple_of(p * 8, 8)
        for q, part in ((3, fold(pixels)), (4, fold(pixels * pixels))):
            s_scr[pl.ds(q * 128 + spot, 8), :] = jnp.broadcast_to(
                jnp.sum(part, axis=0, keepdims=True), (8, 128)
            )
        return carry

    lax.fori_loop(0, P_SIZE, one_sum, 0, unroll=2)
    copy.wait()
    count = springs_ref[GV + seam : GV + seam + 1, 0:1].astype(jnp.int32)
    lane = iota((8, 128), 1)
    full_lane = iota((PATCH, 128), 1)
    row = iota((8, 128), 0)

    def one_patch(p, carry):
        pixels = sent_ref[pl.ds(pl.multiple_of(p * PATCH, PATCH), PATCH), :]
        a_scr[...] = pixels.astype(F32)
        base = (seam * P_SIZE + p) * PITCH
        for s in range(NS):
            move_y = cand_s[0, p * NS + s] + REACH
            top = base + move_y
            move_x = cand_s[1, p * NS + s] + REACH
            crop = jnp.where(
                full_lane < move_x,
                frame_ref[pl.ds(top + WIN, PATCH), :],
                frame_ref[pl.ds(top, PATCH), :],
            )
            cross = fold(pltpu.roll(a_scr[...], move_x, 1) * crop)
            t_scr[9 * s : 9 * s + 8, :] = cross
            at = (seam * P_SIZE + p) * TAB + move_y
            for q in range(2):
                line = jnp.where(
                    full_lane[0:1] < move_x,
                    tab_ref[pl.ds(at + (2 * q + 1) * TOPS, 1), :],
                    tab_ref[pl.ds(at + 2 * q * TOPS, 1), :],
                )
                s_scr[pl.ds((q + 1) * 128 + p * 8 + s, 1), :] = line
        part = t_scr[pl.ds(0, 8, stride=9), :]
        for k in range(1, 8):
            part = part + t_scr[pl.ds(k, 8, stride=9), :]
        s_scr[pl.ds(pl.multiple_of(p * 8, 8), 8), :] = part
        return carry

    lax.fori_loop(0, P_SIZE, one_patch, 0, unroll=8)
    cross, total, square, a_sum, a_sq = (
        jnp.sum(s_scr[128 * q : 128 * q + 128, :].T, axis=0, keepdims=True) / PIXELS
        for q in range(5)
    )
    cov = cross - a_sum * total
    var_a = a_sq - a_sum * a_sum
    var_b = square - total * total
    ncc = cov / jnp.sqrt((var_a + EPSILON) * (var_b + EPSILON))
    weight = jnp.where((lane[0:1] >> 3) < count, (1.5 + ncc) * (1.5 + ncc), 0.0)
    parts = jnp.where(
        row == 0,
        weight,
        jnp.where(row == 1, weight * lists[0:1], jnp.where(row == 2, weight * lists[1:2], 0.0)),
    )
    group = ((iota((128, 128), 0) >> 3) == iota((128, 128), 1)).astype(jnp.bfloat16)
    sums = [jnp.dot(part, group, preferred_element_type=F32) for part in split3(parts)]
    sums = sums[0] + sums[1] + sums[2]

    def estimates(w_sum, w_y, w_x, slot):
        alive = slot < count
        conf = jnp.where(alive, w_sum / NS, 0.0)
        along_y = jnp.where(alive, w_y / (REACH * w_sum), 0.0)
        along_x = jnp.where(alive, w_x / (REACH * w_sum), 0.0)
        return conf, along_y, along_x

    conf, along_y, along_x = estimates(sums[0:1], sums[1:2], sums[2:3], lane[0:1])
    if seam == 1:
        lines = (conf, conf * along_y, conf * along_x, along_y, along_x)
        for k, line in enumerate(lines):
            out_ref[k : k + 1, :] = line
        out_ref[5:8, :] = jnp.zeros((3, 128), F32)
    else:
        lines = (conf, conf * along_y, conf * along_x)
        cols = jnp.concatenate(lines + (jnp.zeros((5, 128), F32),), axis=0).T
        lane16 = iota((16, 128), 1)
        block = springs_ref[0:GV, :]
        for k in range(3):
            block = jnp.where(lane16 == 64 + k, cols[0:16, k : k + 1], block)
        out_ref[0:16, :] = block
        out_ref[16:24, :] = other_ref[...]
        for k, line in enumerate((along_y, along_x, conf)):
            out_ref[21 + k : 22 + k, :] = line


def krylov_kernel(inner_ref, centre_ref, outer_ref, u_ref, mom_ref, match_ref):
    odd = lax.axis_index("col") % 2 == 1
    west = jnp.where(odd, inner_ref[...], outer_ref[...])
    east = jnp.where(odd, outer_ref[...], inner_ref[...])
    tiles = (west, centre_ref[...], east)
    lane = iota((32, 128), 1)
    row = iota((32, 128), 0)
    spans = (slice(8, 16), slice(0, 16), slice(0, 8))
    blocks = [
        jnp.concatenate([tile[a, spans[a], :] for a in range(3)], axis=0) for tile in tiles
    ]

    def both(x):
        return x + pltpu.roll(x, 64, 1)

    def plane(t):
        out = jnp.zeros((32, 128), F32)
        for b in range(3):
            moved = pltpu.roll(blocks[b], (16 * b - 16 * t) % 128, 1)
            out = jnp.where((lane >> 4) == b, moved, out)
        return both(out)

    def west_seam(lane_y, lane_x):
        out = jnp.zeros((32, 128), F32)
        for b in (1, 2):
            out = jnp.where(lane == 16 * b - 1, blocks[b][:, lane_y : lane_y + 1], out)
            out = jnp.where(lane == 16 * b + 63, blocks[b][:, lane_x : lane_x + 1], out)
        return out

    def north_lines(a, r):
        lines = [tile[a, r : r + 1, :] for tile in tiles]
        return lines[0] + pltpu.roll(lines[1], 16, 1) + pltpu.roll(lines[2], 32, 1)

    def north_seam(r_y, r_x):
        out = jnp.zeros((32, 128), F32)
        for a in (1, 2):
            line = north_lines(a, r_y) + pltpu.roll(north_lines(a, r_x), 64, 1)
            out = jnp.where(row == 16 * a - 9, line, out)
        return out

    q_h = plane(0) + west_seam(64, 64)
    q_v = plane(1) + north_seam(16, 16)
    q_d = plane(2)
    q_a = plane(3)
    f_h = west_seam(65, 66)
    f_v = north_seam(17, 18)

    def right(x):
        return pltpu.roll(x, 1, 1)

    def left(x):
        return pltpu.roll(x, 127, 1)

    def down(x):
        return pltpu.roll(x, 1, 0)

    def up(x):
        return pltpu.roll(x, 31, 0)

    from_west, from_above = right(q_h), down(q_v)
    from_corner, from_other = down(right(q_d)), down(left(q_a))
    own_q = (LAMBDA_REG - THETA) + (q_h + from_west) + (q_v + from_above)
    own_q = own_q + (q_d + from_corner) + (q_a + from_other)

    def operate(v):
        above, below = down(v), up(v)
        out = own_q * v - q_v * below - from_above * above
        out = out - (q_h * left(v) + from_west * right(v))
        out = out - (q_d * left(below) + from_corner * right(above))
        return out - (q_a * right(below) + from_other * left(above))

    u0 = f_h + f_v - right(f_h) - down(f_v)
    u1 = operate(u0)
    u2 = operate(u1)
    u3 = operate(u2)
    own = slice(8, 24)
    lane16 = lane[own]
    inside = ((lane16 >= 16) & (lane16 < 32)) | ((lane16 >= 80) & (lane16 < 96))
    parts = [jnp.where(inside, x[own], 0.0) for x in (u0, u1, u2, u3)]
    lane1 = iota((1, 128), 1)
    moments = jnp.zeros((1, 128), F32)
    for k in range(6):
        product = parts[k // 2] * parts[k // 2 + k % 2]
        value = jnp.sum(jnp.sum(product, axis=0, keepdims=True), axis=1, keepdims=True)
        moments = jnp.where(lane1 == k, value, moments)
    for k in range(3):
        u_ref[k] = parts[k]
    mom_ref[...] = jnp.broadcast_to(moments[None], mom_ref.shape)
    for k, (east_row, south_row) in enumerate(((21, 19), (22, 20), (23, 16))):
        match_ref[k, 0:1, :] = east[1, east_row : east_row + 1, 0:16]
        match_ref[k, 1:2, :] = centre_ref[2, south_row : south_row + 1, 0:16]


def flatten_kernel(u_ref, out_ref):
    vertex = iota((128, 256), 1)
    source = iota((128, 256), 0)
    fields = jnp.concatenate([u_ref[k] for k in range(3)], axis=0)
    keep = iota((16, 256), 0) == (iota((16, 256), 1) >> 4)
    for comp in range(2):
        spread = (source == (vertex & 15) + (16 + 64 * comp)).astype(F32)
        wide = jnp.dot(fields, spread, precision=PRECISE, preferred_element_type=F32)
        for k in range(3):
            line = jnp.where(keep, wide[16 * k : 16 * k + 16], 0.0)
            out_ref[k, comp : comp + 1, :] = jnp.sum(line, axis=0, keepdims=True)


def combine_kernel(mom_ref, u_ref, out_ref):
    total = jnp.sum(mom_ref[...], axis=0, keepdims=True)
    lane = iota((1, 128), 1)
    m = [
        jnp.broadcast_to(
            jnp.sum(jnp.where(lane == k, total, 0.0), axis=1, keepdims=True), (1, 128)
        )
        for k in range(6)
    ]

    def gram(p, lift):
        out = None
        for i in range(3):
            for j in range(i, 3):
                if p[i] is None or p[j] is None:
                    continue
                term = m[i + j]
                if lift:
                    term = m[i + j + 1] + THETA * term
                term = (term * p[i]) * p[j]
                if j > i:
                    term = term + term
                out = term if out is None else out + term
        return out

    one = jnp.ones((1, 128), F32)
    r = [one, None, None]
    d = r
    rr = m[0]
    x = [None, None, None]

    def plus(a, b):
        return b if a is None else a if b is None else a + b

    def times(s, a):
        return None if a is None else s * a

    for step in range(3):
        alpha = rr / gram(d, True)
        x = [plus(x[i], times(alpha, d[i])) for i in range(3)]
        if step == 2:
            break
        image = [times(THETA, d[0]), plus(d[0], times(THETA, d[1])), plus(d[1], times(THETA, d[2]))]
        r = [plus(r[i], times(-alpha, image[i])) for i in range(3)]
        new = gram(r, False)
        d = [plus(r[i], times(new / rr, d[i])) for i in range(3)]
        rr = new
    wide = [jnp.concatenate([c, c], axis=1) for c in x]
    out_ref[...] = wide[0] * u_ref[0] + wide[1] * u_ref[1] + wide[2] * u_ref[2]


def limit(mib):
    return pltpu.CompilerParams(vmem_limit_bytes=mib * 1024 * 1024)


def shape(dims, dtype=F32):
    return jax.ShapeDtypeStruct(dims, dtype)


def swaps(x, axis):
    length = lax.axis_size(axis)
    inner = [(i, i ^ 1) for i in range(length)]
    outer = [(i, i + 1 if i % 2 else i - 1) for i in range(1, length - 1)]
    return lax.ppermute(x, axis, inner), lax.ppermute(x, axis, outer)


def call_pack(patches, candidates):
    return pl.pallas_call(
        pack_kernel,
        out_shape=tuple(
            shape((P_SIZE * PATCH + tail, 128), jnp.bfloat16) for tail in (32, 16)
        ),
        in_specs=[HBM, VMEM],
        out_specs=(VMEM, VMEM),
        scratch_shapes=[pltpu.SemaphoreType.DMA((2,))],
        compiler_params=limit(4),
    )(patches, candidates)


def call_frames(windows):
    return pl.pallas_call(
        frames_kernel,
        out_shape=(shape((2 * P_SIZE * PITCH, 128)), shape((2 * P_SIZE * TAB, 128))),
        in_specs=[VMEM],
        out_specs=(VMEM, VMEM),
        compiler_params=limit(16),
    )(windows)


def call_match(seam, *operands):
    return pl.pallas_call(
        functools.partial(match_kernel, seam),
        out_shape=shape((24 if seam == 0 else 8, 128)),
        in_specs=[VMEM] * len(operands),
        out_specs=VMEM,
        scratch_shapes=[
            pltpu.VMEM((128, 128), F32),
            pltpu.VMEM((72, 128), F32),
            pltpu.VMEM((640, 128), F32),
            pltpu.VMEM((8, 128), jnp.int32),
            pltpu.SMEM((8, 128), jnp.int32),
            pltpu.SemaphoreType.DMA,
        ],
        compiler_params=limit(14),
    )(*operands)


def body(patches, windows, candidates, live, edges, stiffness):
    to_east, to_south = call_pack(patches.reshape(2, P_SIZE * PATCH, PATCH), candidates[0, 0])
    sent_west = shifted(to_east, "col", 1)
    sent_north = shifted(to_south, "row", 1)

    frames, table = call_frames(windows[0, 0])
    springs = pl.pallas_call(
        springs_kernel,
        out_shape=shape((GV + 8, 128)),
        in_specs=[VMEM, VMEM, VMEM],
        out_specs=VMEM,
        scratch_shapes=[pltpu.VMEM((8, E_PAD), jnp.int32), pltpu.VMEM((8, E_PAD), F32)],
        compiler_params=limit(4),
    )(edges[0], stiffness, live.transpose(0, 2, 1))
    seam_north = call_match(1, springs, sent_north, frames, table)
    own = call_match(0, springs, sent_west, frames, table, seam_north)
    inner, outer = swaps(own, "row")
    odd = lax.axis_index("row") % 2 == 1
    centre = jnp.stack([jnp.where(odd, inner, outer), own, jnp.where(odd, outer, inner)])
    inner, outer = swaps(centre, "col")
    devices = lax.axis_size("row") * lax.axis_size("col")
    basis, moments, matches = pl.pallas_call(
        krylov_kernel,
        out_shape=(shape((3, 16, 128)), shape((devices, 1, 128)), shape((3, 2, P_SIZE))),
        in_specs=[VMEM] * 3,
        out_specs=(VMEM, VMEM, VMEM),
        compiler_params=limit(4),
    )(inner, centre, outer)
    moments = lax.all_to_all(moments, ("row", "col"), 0, 0).reshape(devices, 128)
    flat = pl.pallas_call(
        flatten_kernel,
        out_shape=shape((3, 2, GV * GV)),
        in_specs=[VMEM],
        out_specs=VMEM,
        compiler_params=limit(4),
    )(basis)
    mesh_shift = pl.pallas_call(
        combine_kernel,
        out_shape=shape((2, GV * GV)),
        in_specs=[VMEM, VMEM],
        out_specs=VMEM,
        compiler_params=limit(4),
    )(moments, flat)
    return matches.transpose(1, 0, 2)[None, None], mesh_shift[None, None]


def solution(mesh):
    return jax.shard_map(
        body,
        mesh=mesh,
        in_specs=(
            P("row", "col", None, None, None, None),
            P("row", "col", None, None, None),
            P("row", "col", None, None, None),
            P(),
            P("row", None, "col"),
            P("row", "col"),
        ),
        out_specs=(P("row", "col", None, None, None), P("row", "col", None, None)),
        check_vma=False,
    )
```
